512 devices in a mesh: dp: 32 (over z, core), ctx: 16 (over x, y).
Axes of the slice: x: 4, y: 4, z: 16, core: 2. Of those that a mesh axis runs over, the one named last changes fastest.
Arguments:
- queries: bfloat16 [65536, 1024], P(('dp', 'ctx')), may hold values from -6 to 6
- key_vectors: bfloat16 [65536, 1024], P(('dp', 'ctx')), may hold values from -6 to 6
- value_vectors: bfloat16 [65536, 1024], P(('dp', 'ctx')), may hold values from -6 to 6
- gate_values: bfloat16 [65536, 1024], P(('dp', 'ctx')), may hold values from -6 to 6
- cotangent: bfloat16 [65536, 1024], P(('dp', 'ctx')), may hold values from -6 to 6
- norm_gain: float32 [1024], replicated, may hold values from 0.5 to 1.5
- lengths: int32 [32, 4], P('dp'), may hold values from 1 to 1024, 2048 in all within a row
Outputs:
- output: bfloat16 [65536, 1024], P(('dp', 'ctx'))
- grad_queries: bfloat16 [65536, 1024], P(('dp', 'ctx'))
- grad_keys: bfloat16 [65536, 1024], P(('dp', 'ctx'))
- grad_values: bfloat16 [65536, 1024], P(('dp', 'ctx'))
- grad_gain: float32 [1024], replicated
The draws below stay inside these ranges and needn't reach their ends.
Inputs may be any that keep to these rules, and one draw needn't show every extreme that they name: Each group's lengths sum to 2048, and the longest is exactly half of that.
All inputs are finite; a program needn't handle non-finite values.
Results may differ from the reference program's by a relative error of at most 0.0058.
Values may be sent and summed in bfloat16 or wider, within the bound.
A program may use at most 128 MiB of HBM per device.

```python
import math
import jax
import jax.numpy as jnp
import numpy as np
from jax import lax

HEAD = 128
ROWS = 128
USERS = 4
WIDTH = 1024
GROUPS = 32
TOKENS = 65536
N_CTX = 16


def shard_levels(stream_key, dims, shards, least, high):
    factor_of, own = 1.0, jax.random.fold_in(stream_key, 6)
    for position, parts in shards:
        heights = jnp.exp(jax.random.uniform(jax.random.fold_in(own, position), (parts,), jnp.float32, least / len(shards), high / len(shards)))
        factor_of = factor_of * jnp.repeat(heights, dims[position] // parts).reshape([-1 if axis == position else 1 for axis in range(len(dims))])
    return factor_of


def profile(amount, total, limit, lean):
    weights = [(1 << 20) // math.isqrt(standing ** lean) + 1 for standing in range(2, amount + 1)]
    spare, counts = total - limit - (amount - 1), [1] * (amount - 1)
    while spare > 0:
        candidates = [i for i in range(amount - 1) if counts[i] < limit]
        mass, remaining = sum([weights[i] for i in candidates]), spare
        for i in candidates:
            extra = min(limit - counts[i], max(1, remaining * weights[i] // mass), spare)
            counts[i] = counts[i] + extra
            spare = spare - extra
    return np.array([limit] + counts)


def uneven_parts(rng, number_of, total, reach, lean):
    if number_of == 2:
        one = jax.random.randint(rng, (), max(1, total - reach), min(reach, total - 1) + 1)
        return jnp.stack([one, total - one])
    sizes = jnp.asarray(profile(number_of, total, reach, lean), jnp.int32)
    couples = (number_of - 1) // 2
    giver, taker = sizes[1:1 + 2 * couples:2], sizes[2:2 + 2 * couples:2]
    margin = jnp.minimum(giver - 1, reach - taker)
    passed = jax.random.randint(jax.random.fold_in(rng, 1), (couples,), 0, 1 << 20) % (margin + 1)
    sizes = sizes.at[1:1 + 2 * couples:2].set(giver - passed).at[2:2 + 2 * couples:2].set(taker + passed)
    return sizes[jax.random.permutation(jax.random.fold_in(rng, 2), number_of)]


def gaussian(stream_key, extent, deviation, reach, pieces=(), kind=jnp.bfloat16):
    values = jax.random.normal(stream_key, extent, jnp.float32) * deviation
    if len(pieces) > 0:
        values = shard_levels(stream_key, extent, pieces, -0.22, 0.18) * values
    return jnp.clip(values, min=-reach, max=reach).astype(kind)


def setup_inputs(seed: int = 0) -> dict:
    arg_keys = jax.random.split(jax.random.key(seed), 8)
    return {
        "queries": gaussian(arg_keys[0], (TOKENS, WIDTH), 1.0, 6.0, ((0, 512),)),
        "key_vectors": gaussian(arg_keys[1], (TOKENS, WIDTH), 1.0, 6.0, ((0, 512),)),
        "value_vectors": gaussian(arg_keys[2], (TOKENS, WIDTH), 1.0, 6.0, ((0, 512),)),
        "gate_values": gaussian(arg_keys[3], (TOKENS, WIDTH), 1.0, 6.0, ((0, 512),)),
        "cotangent": gaussian(arg_keys[4], (TOKENS, WIDTH), 1.0, 6.0, ((0, 512),)),
        "norm_gain": jnp.clip(1.0 + 0.1 * jax.random.normal(arg_keys[5], (WIDTH,), jnp.float32), 0.5, 1.5),
        "lengths": jax.vmap(lambda own: uneven_parts(own, USERS, ROWS * N_CTX, ROWS * N_CTX // 2, 2))(jax.random.split(arg_keys[6], GROUPS)).reshape((GROUPS, USERS)).astype(jnp.int32),
    }


EPSILON = 1e-05

def event_time(rows, row_count, shard_count):
    half = row_count // 2
    shard = rows // row_count
    local = rows % row_count
    early = shard * half + local
    late = (2 * shard_count - 1 - shard) * half + local - half
    return jnp.where(local < half, early, late).astype(jnp.int32)

def user_index(positions, user_ends):
    return lax.optimization_barrier(jnp.sum((positions[:, None] >= user_ends[None, :]).astype(jnp.int32), axis=1))

def pair_mask(query_pos, key_pos, user_ends):
    same = user_index(query_pos, user_ends)[:, None] == user_index(key_pos, user_ends)[None, :]
    before = key_pos[None, :] <= query_pos[:, None]
    return jnp.where(same & before, 1.0, 0.0).astype(jnp.float32)

def head_split(matrix):
    return matrix.astype(jnp.float32).reshape(matrix.shape[0], -1, HEAD)

def head_scores(left, right):
    return jnp.einsum('rhd,chd->hrc', head_split(left), head_split(right)) / math.sqrt(HEAD)

def silu_slope(scores):
    sigmoid = jax.nn.sigmoid(scores)
    return sigmoid * (1.0 + scores * (1.0 - sigmoid))

def one_group(queries, key_vectors, value_vectors, gate_values, cotangent, group_lengths, norm_gain):
    row_total = queries.shape[0]
    block_rows = min(ROWS, 512)
    block_count = row_total // block_rows
    user_ends = jnp.cumsum(group_lengths).astype(jnp.int32)
    positions = event_time(jnp.arange(row_total, dtype=jnp.int32), ROWS, N_CTX)

    def forward_block(block_index):
        begin = (block_index * block_rows).astype(jnp.int32)
        query_pos = lax.dynamic_slice_in_dim(positions, begin, block_rows, 0)
        query_block = lax.dynamic_slice_in_dim(queries, begin, block_rows, 0)
        scores = head_scores(query_block, key_vectors)
        weights = (jax.nn.silu(scores) * pair_mask(query_pos, positions, user_ends)[None]).astype(jnp.bfloat16)
        result = jnp.einsum('hrc,chd->rhd', weights.astype(jnp.float32), head_split(value_vectors))
        return result.reshape(block_rows, -1)
    block_ids = jnp.arange(block_count, dtype=jnp.int32)
    attended = lax.map(forward_block, block_ids).reshape(row_total, -1)
    row_mean = lax.optimization_barrier(jnp.mean(attended, axis=1, keepdims=True))
    centered = attended - row_mean
    variance = lax.optimization_barrier(jnp.mean(centered * centered, axis=1, keepdims=True))
    inverse = lax.rsqrt(variance + EPSILON)
    normed = centered * inverse
    gates = gate_values.astype(jnp.float32)
    grads = cotangent.astype(jnp.float32)
    scaled_gates = gates * norm_gain.astype(jnp.float32)[None, :]
    output = (normed * scaled_gates).astype(jnp.bfloat16)
    gain_part = lax.optimization_barrier(jnp.sum(normed * grads * gates, axis=0))
    grad_norm = grads * scaled_gates
    grad_attended = ((grad_norm - lax.optimization_barrier(jnp.mean(grad_norm, axis=1, keepdims=True)) - normed * lax.optimization_barrier(jnp.mean(grad_norm * normed, axis=1, keepdims=True))) * inverse).astype(jnp.bfloat16)

    def query_block(block_index):
        begin = (block_index * block_rows).astype(jnp.int32)
        query_pos = lax.dynamic_slice_in_dim(positions, begin, block_rows, 0)
        query_part = lax.dynamic_slice_in_dim(queries, begin, block_rows, 0)
        grad_part = lax.dynamic_slice_in_dim(grad_attended, begin, block_rows, 0)
        scores = head_scores(query_part, key_vectors)
        live = pair_mask(query_pos, positions, user_ends)[None]
        grad_weights = jnp.einsum('rhd,chd->hrc', head_split(grad_part), head_split(value_vectors))
        grad_scores = (grad_weights * silu_slope(scores) * live / math.sqrt(HEAD)).astype(jnp.bfloat16)
        result = jnp.einsum('hrc,chd->rhd', grad_scores.astype(jnp.float32), head_split(key_vectors))
        return result.reshape(block_rows, -1)

    def key_block(block_index):
        begin = (block_index * block_rows).astype(jnp.int32)
        key_pos = lax.dynamic_slice_in_dim(positions, begin, block_rows, 0)
        key_part = lax.dynamic_slice_in_dim(key_vectors, begin, block_rows, 0)
        value_part = lax.dynamic_slice_in_dim(value_vectors, begin, block_rows, 0)
        scores = head_scores(queries, key_part)
        live = pair_mask(positions, key_pos, user_ends)[None]
        weights = (jax.nn.silu(scores) * live).astype(jnp.bfloat16)
        grad_weights = jnp.einsum('rhd,chd->hrc', head_split(grad_attended), head_split(value_part))
        grad_scores = (grad_weights * silu_slope(scores) * live / math.sqrt(HEAD)).astype(jnp.bfloat16)
        grad_value = jnp.einsum('hrc,rhd->chd', weights.astype(jnp.float32), head_split(grad_attended))
        grad_key = jnp.einsum('hrc,rhd->chd', grad_scores.astype(jnp.float32), head_split(queries))
        return (grad_key.reshape(block_rows, -1), grad_value.reshape(block_rows, -1))
    grad_queries = lax.map(query_block, block_ids).reshape(row_total, -1).astype(jnp.bfloat16)
    grad_key_blocks, grad_value_blocks = lax.map(key_block, block_ids)
    grad_keys = grad_key_blocks.reshape(row_total, -1).astype(jnp.bfloat16)
    grad_values = grad_value_blocks.reshape(row_total, -1).astype(jnp.bfloat16)
    return (output, grad_queries, grad_keys, grad_values, gain_part)

def reference(queries, key_vectors, value_vectors, gate_values, cotangent, norm_gain, lengths):
    group_rows = ROWS * N_CTX

    def regroup(matrix):
        return matrix.reshape(GROUPS, group_rows, -1)

    def per_group(packed):
        return one_group(packed[0], packed[1], packed[2], packed[3], packed[4], packed[5], norm_gain)
    output, grad_queries, grad_keys, grad_values, gain_parts = lax.map(per_group, (regroup(queries), regroup(key_vectors), regroup(value_vectors), regroup(gate_values), regroup(cotangent), lengths))
    grad_gain = lax.optimization_barrier(jnp.sum(gain_parts, axis=0))
    return (output.reshape(TOKENS, -1), grad_queries.reshape(TOKENS, -1), grad_keys.reshape(TOKENS, -1), grad_values.reshape(TOKENS, -1), grad_gain)
```

```python
import functools
import math

import jax
import jax.numpy as jnp
from jax import lax
from jax.experimental import pallas as pl
from jax.experimental.pallas import tpu as pltpu
from jax.sharding import PartitionSpec as P

HEAD = 128
EPSILON = 1e-05
PEERS = 16
CHUNK = 64
HALF = PEERS * CHUNK
BLOCK = 256
WINDOW = HALF + BLOCK
STEPS = HALF // BLOCK
SCALE = 1.0 / math.sqrt(HEAD)

QUERY, KEY_E, KEY_L, VAL_E, VAL_L, ATT, GRAD, DQ, DK_E, DK_L, DV_E, DV_L = range(12)
KINDS = 12


def contract(left, right, left_axis, right_axis):
    return lax.dot_general(
        left, right, (((left_axis,), (right_axis,)), ((), ())), preferred_element_type=jnp.float32
    )


def attention_kernel(
    lengths,
    queries,
    keys,
    values,
    gates,
    cotangent,
    gain,
    output,
    grad_queries,
    grad_keys,
    grad_values,
    gain_part,
    q_all,
    k_all,
    v_all,
    weights,
    slopes,
    att_out,
    att_in,
    grad_out,
    grad_in,
    dq_out,
    dq_in,
    dk_sum,
    dv_sum,
    dk_out,
    dv_out,
    dk_early,
    dk_late,
    dv_early,
    dv_late,
    send_sem,
    recv_sem,
):
    me = lax.axis_index("ctx")
    head = me // 2
    role = me % 2

    def columns(which):
        return pl.ds(pl.multiple_of(which * HEAD, HEAD), HEAD)

    def rows_at(start, size=CHUNK):
        return pl.ds(pl.multiple_of(start, CHUNK), size)

    def remote(src, dst, kind, target, source):
        return pltpu.make_async_remote_copy(
            src_ref=src,
            dst_ref=dst,
            send_sem=send_sem.at[kind, target],
            recv_sem=recv_sem.at[kind, source],
            device_id={"ctx": target},
            device_id_type=pl.DeviceIdType.MESH,
        )

    def push(src, dst, kind, target):
        @pl.when(target != me)
        def _():
            remote(src, dst, kind, target, me).start()

        @pl.when(target == me)
        def _():
            dst[...] = src[...]

    def arrived(buffer, kind, source):
        @pl.when(source != me)
        def _():
            remote(buffer, buffer, kind, source, source).wait_recv()

    def sent(buffer, kind, target):
        @pl.when(target != me)
        def _():
            remote(buffer, buffer, kind, target, me).wait_send()

    def each_peer(work):
        def step(turn, carry):
            work(lax.rem(me + turn, PEERS))
            return carry

        lax.fori_loop(0, PEERS, step, 0)

    barrier = pltpu.get_barrier_semaphore()

    def greet(turn, carry):
        pl.semaphore_signal(
            barrier,
            inc=1,
            device_id={"ctx": lax.rem(me + turn, PEERS)},
            device_id_type=pl.DeviceIdType.MESH,
        )
        return carry

    lax.fori_loop(1, PEERS, greet, 0)

    @pl.when(role == 0)
    def _():
        k_all[:HALF, :] = jnp.zeros((HALF, HEAD), jnp.bfloat16)
        v_all[:HALF, :] = jnp.zeros((HALF, HEAD), jnp.bfloat16)

    pl.semaphore_wait(barrier, PEERS - 1)

    def chunk_of(shard, kind_role):
        return jnp.where(kind_role == 0, shard, PEERS - 1 - shard)

    piece = q_all.at[:CHUNK, :]

    def send_queries_keys(peer):
        peer_role, cols = peer % 2, columns(peer // 2)
        push(
            queries.at[rows_at(peer_role * CHUNK), cols],
            q_all.at[rows_at(chunk_of(me, peer_role) * CHUNK), :],
            QUERY,
            peer,
        )
        push(
            keys.at[:CHUNK, cols],
            k_all.at[rows_at(me * CHUNK + (1 - peer_role) * HALF), :],
            KEY_E,
            peer,
        )

        @pl.when(peer_role == 1)
        def _():
            push(
                keys.at[CHUNK:, cols],
                k_all.at[rows_at((2 * PEERS - 1 - me) * CHUNK), :],
                KEY_L,
                peer,
            )

    def send_values(peer):
        peer_role, cols = peer % 2, columns(peer // 2)
        push(
            values.at[:CHUNK, cols],
            v_all.at[rows_at(me * CHUNK + (1 - peer_role) * HALF), :],
            VAL_E,
            peer,
        )

        @pl.when(peer_role == 1)
        def _():
            push(
                values.at[CHUNK:, cols],
                v_all.at[rows_at((2 * PEERS - 1 - me) * CHUNK), :],
                VAL_L,
                peer,
            )

    each_peer(send_queries_keys)
    each_peer(send_values)

    def wait_queries_keys(peer):
        arrived(piece, QUERY, peer)
        arrived(piece, KEY_E, peer)

        @pl.when(role == 1)
        def _():
            arrived(piece, KEY_L, peer)

    def wait_values(peer):
        arrived(piece, VAL_E, peer)

        @pl.when(role == 1)
        def _():
            arrived(piece, VAL_L, peer)

    each_peer(wait_queries_keys)

    ends = []
    total = 0
    for user in range(lengths.shape[1]):
        total = total + lengths[0, user]
        ends.append(total)

    def score_step(step, carry):
        rows = pl.ds(pl.multiple_of(step * BLOCK, BLOCK), BLOCK)
        q_block = q_all[rows, :]
        q_time = role * HALF + step * BLOCK + lax.broadcasted_iota(jnp.int32, (BLOCK, 1), 0)
        first = jnp.zeros((BLOCK, 1), jnp.int32)
        for end in ends:
            first = jnp.where(q_time >= end, end, first)
        for part in range(WINDOW // BLOCK):
            start = step * BLOCK + part * BLOCK
            k_block = k_all[pl.ds(pl.multiple_of(start, BLOCK), BLOCK), :]
            k_time = (
                start - (1 - role) * HALF + lax.broadcasted_iota(jnp.int32, (1, BLOCK), 1)
            )
            scores = contract(q_block, k_block, 1, 1) * SCALE
            live = (k_time >= first) & (k_time <= q_time)
            sigmoid = 0.5 * jnp.tanh(0.5 * scores) + 0.5
            silu = scores * sigmoid
            slope = (sigmoid + silu * (1.0 - sigmoid)) * SCALE
            cols = slice(part * BLOCK, (part + 1) * BLOCK)
            weights[rows, cols] = jnp.where(live, silu, 0.0).astype(jnp.bfloat16)
            slopes[rows, cols] = jnp.where(live, slope, 0.0)
        return carry

    lax.fori_loop(0, STEPS, score_step, 0)

    each_peer(wait_values)

    def attend_step(step, carry):
        rows = pl.ds(pl.multiple_of(step * BLOCK, BLOCK), BLOCK)
        window = pl.ds(pl.multiple_of(step * BLOCK, BLOCK), WINDOW)
        att_out[rows, :] = contract(weights[rows, :], v_all[window, :], 1, 0).astype(jnp.bfloat16)
        for part in range(BLOCK // CHUNK):
            chunk = step * (BLOCK // CHUNK) + part
            push(
                att_out.at[rows_at(chunk * CHUNK), :],
                att_in.at[rows_at(role * CHUNK), columns(head)],
                ATT,
                chunk_of(chunk, role),
            )
        return carry

    lax.fori_loop(0, STEPS, attend_step, 0)

    gain_row = gain[...]
    gain_sum = jnp.zeros((1, gain.shape[1]), jnp.float32)
    each_peer(lambda peer: arrived(piece, ATT, peer))
    for part in range(4):
        rows = slice(part * 32, part * 32 + 32)
        attended = att_in[rows, :].astype(jnp.float32)
        centered = attended - jnp.mean(attended, axis=1, keepdims=True)
        variance = jnp.mean(centered * centered, axis=1, keepdims=True)
        inverse = lax.rsqrt(variance + EPSILON)
        normed = centered * inverse
        gate = gates[rows, :].astype(jnp.float32)
        grad = cotangent[rows, :].astype(jnp.float32)
        scaled = gate * gain_row
        output[rows, :] = (normed * scaled).astype(jnp.bfloat16)
        gain_sum = gain_sum + jnp.sum(normed * grad * gate, axis=0, keepdims=True)
        grad = grad * scaled
        grad_out[rows, :] = (
            (
                grad
                - jnp.mean(grad, axis=1, keepdims=True)
                - normed * jnp.mean(grad * normed, axis=1, keepdims=True)
            )
            * inverse
        ).astype(jnp.bfloat16)
    gain_part[...] = gain_sum

    def send_grad(peer):
        peer_role = peer % 2
        push(
            grad_out.at[rows_at(peer_role * CHUNK), columns(peer // 2)],
            grad_in.at[rows_at(chunk_of(me, peer_role) * CHUNK), :],
            GRAD,
            peer,
        )

    each_peer(send_grad)
    dk_sum[...] = jnp.zeros(dk_sum.shape, jnp.float32)
    dv_sum[...] = jnp.zeros(dv_sum.shape, jnp.float32)

    def backward_step(turn, carry):
        step = STEPS - 1 - turn
        for part in range(BLOCK // CHUNK):
            arrived(piece, GRAD, chunk_of(step * (BLOCK // CHUNK) + part, role))
        rows = pl.ds(pl.multiple_of(step * BLOCK, BLOCK), BLOCK)
        grad = grad_in[rows, :]
        q_block = q_all[rows, :]
        dq = jnp.zeros((BLOCK, HEAD), jnp.float32)
        for part in range(WINDOW // BLOCK):
            window = pl.ds(pl.multiple_of(step * BLOCK + part * BLOCK, BLOCK), BLOCK)
            cols = slice(part * BLOCK, (part + 1) * BLOCK)
            grad_weights = contract(grad, v_all[window, :], 1, 1)
            grad_scores = (grad_weights * slopes[rows, cols]).astype(jnp.bfloat16)
            dq = dq + contract(grad_scores, k_all[window, :], 1, 0)
            dk_sum[window, :] += contract(grad_scores, q_block, 0, 0)
            dv_sum[window, :] += contract(weights[rows, cols], grad, 0, 0)
        dq_out[rows, :] = dq.astype(jnp.bfloat16)
        for part in range(BLOCK // CHUNK):
            chunk = step * (BLOCK // CHUNK) + part
            push(
                dq_out.at[rows_at(chunk * CHUNK), :],
                dq_in.at[rows_at(role * CHUNK), columns(head)],
                DQ,
                chunk_of(chunk, role),
            )
        return carry

    lax.fori_loop(0, STEPS, backward_step, 0)
    dk_out[...] = dk_sum[...].astype(jnp.bfloat16)
    dv_out[...] = dv_sum[...].astype(jnp.bfloat16)

    def send_key_grads(peer):
        early = rows_at(peer * CHUNK + (1 - role) * HALF)
        slot = rows_at(role * CHUNK)
        push(dk_out.at[early, :], dk_early.at[slot, columns(head)], DK_E, peer)
        push(dv_out.at[early, :], dv_early.at[slot, columns(head)], DV_E, peer)

        @pl.when(role == 1)
        def _():
            late = rows_at((2 * PEERS - 1 - peer) * CHUNK)
            push(dk_out.at[late, :], dk_late.at[:, columns(head)], DK_L, peer)
            push(dv_out.at[late, :], dv_late.at[:, columns(head)], DV_L, peer)

    each_peer(send_key_grads)

    each_peer(lambda peer: arrived(piece, DQ, peer))
    grad_queries[...] = dq_in[...]

    def wait_key_grads(peer):
        arrived(piece, DK_E, peer)
        arrived(piece, DV_E, peer)

        @pl.when(peer % 2 == 1)
        def _():
            arrived(piece, DK_L, peer)
            arrived(piece, DV_L, peer)

    each_peer(wait_key_grads)

    def summed(early):
        return (early[:CHUNK, :].astype(jnp.float32) + early[CHUNK:, :].astype(jnp.float32)).astype(
            jnp.bfloat16
        )

    grad_keys[:CHUNK, :] = summed(dk_early)
    grad_keys[CHUNK:, :] = dk_late[...]
    grad_values[:CHUNK, :] = summed(dv_early)
    grad_values[CHUNK:, :] = dv_late[...]

    def drain(peer):
        for kind in (QUERY, KEY_E, VAL_E, ATT, GRAD, DQ, DK_E, DV_E):
            sent(piece, kind, peer)

        @pl.when(peer % 2 == 1)
        def _():
            sent(piece, KEY_L, peer)
            sent(piece, VAL_L, peer)

        @pl.when(role == 1)
        def _():
            sent(piece, DK_L, peer)
            sent(piece, DV_L, peer)

    each_peer(drain)


def body(queries, key_vectors, value_vectors, gate_values, cotangent, norm_gain, lengths):
    row_count, width = queries.shape
    wide = jax.ShapeDtypeStruct((row_count, width), jnp.bfloat16)
    vmem = pl.BlockSpec(memory_space=pltpu.VMEM)
    half16 = pltpu.VMEM((HALF, HEAD), jnp.bfloat16)
    full16 = pltpu.VMEM((2 * HALF, HEAD), jnp.bfloat16)
    full32 = pltpu.VMEM((2 * HALF, HEAD), jnp.float32)
    rows16 = pltpu.VMEM((row_count, width), jnp.bfloat16)
    chunk16 = pltpu.VMEM((CHUNK, width), jnp.bfloat16)
    output, grad_queries, grad_keys, grad_values, gain_part = pl.pallas_call(
        attention_kernel,
        out_shape=(wide, wide, wide, wide, jax.ShapeDtypeStruct((1, width), jnp.float32)),
        in_specs=[pl.BlockSpec(memory_space=pltpu.SMEM)] + [vmem] * 6,
        out_specs=(vmem,) * 5,
        scratch_shapes=[
            half16,
            full16,
            full16,
            pltpu.VMEM((HALF, WINDOW), jnp.bfloat16),
            pltpu.VMEM((HALF, WINDOW), jnp.float32),
            half16,
            rows16,
            rows16,
            half16,
            half16,
            rows16,
            full32,
            full32,
            full16,
            full16,
            rows16,
            chunk16,
            rows16,
            chunk16,
            pltpu.SemaphoreType.DMA((KINDS, PEERS)),
            pltpu.SemaphoreType.DMA((KINDS, PEERS)),
        ],
        compiler_params=pltpu.CompilerParams(
            collective_id=0, has_side_effects=True, vmem_limit_bytes=48 * 2**20
        ),
    )(lengths, queries, key_vectors, value_vectors, gate_values, cotangent, norm_gain.reshape(1, width))
    grad_gain = lax.psum(gain_part[0], ("dp", "ctx"))
    return output, grad_queries, grad_keys, grad_values, grad_gain


def solution(mesh):
    rows = P(("dp", "ctx"), None)
    return jax.shard_map(
        body,
        mesh=mesh,
        in_specs=(rows,) * 5 + (P(), P("dp", None)),
        out_specs=(rows,) * 4 + (P(),),
        check_vma=False,
    )
```

```python
import math

import jax
import jax.numpy as jnp
from jax import lax
from jax.experimental import pallas as pl
from jax.experimental.pallas import tpu as pltpu
from jax.sharding import PartitionSpec as P

HEAD = 128
EPSILON = 1e-05
PEERS = 16
HEADS = 8
CHUNK = 64
HALF = PEERS * CHUNK
BLOCK = 256
PER_BLOCK = BLOCK // CHUNK
STEPS = HALF // BLOCK
PARTS = STEPS + 1
SCALE = 1.0 / math.sqrt(HEAD)
STAGGER = True

QUERY, KEY, VALUE, ATT, GRAD, BACK, BACK_E, GAIN = range(8)
KINDS = 8
MESH = pl.DeviceIdType.MESH


def contract(left, right, left_axis, right_axis):
    return lax.dot_general(
        left, right, (((left_axis,), (right_axis,)), ((), ())), preferred_element_type=jnp.float32
    )


def gain_stages(groups):
    stages, stride, slot = [], 1, PEERS
    while stride < groups:
        size = min(4, groups // stride)
        stages.append((slot, stride, size))
        slot, stride = slot + size, stride * size
    return stages, slot


def attention_kernel(
    groups,
    lengths_hbm,
    queries_hbm,
    keys_hbm,
    values_hbm,
    gates_hbm,
    cotangent_hbm,
    gain_hbm,
    output,
    grad_queries,
    grad_keys,
    grad_values,
    gain_total,
    lengths,
    own,
    gates,
    cotangent,
    gain,
    box,
    weights,
    slopes,
    att_out,
    att_in,
    grad_out,
    grad_in,
    sums,
    out_box,
    back_early,
    back_late,
    gain_slots,
    local_sem,
    send_sem,
    recv_sem,
    gain_send_sem,
    gain_recv_sem,
    go_sem,
):
    me = lax.axis_index("ctx")
    group = lax.axis_index("dp")
    core = group % 2
    head = me // 2
    role = (me + core) % 2
    stages, _ = gain_stages(groups)

    staged = [
        pltpu.make_async_copy(src, dst, local_sem.at[index])
        for index, (src, dst) in enumerate(
            (
                (queries_hbm, own.at[0]),
                (keys_hbm, own.at[1]),
                (values_hbm, own.at[2]),
                (lengths_hbm, lengths),
                (gates_hbm, gates),
                (cotangent_hbm, cotangent),
                (gain_hbm, gain),
            )
        )
    ]
    for copy in staged:
        copy.start()

    def columns(which):
        return pl.ds(pl.multiple_of(which * HEAD, HEAD), HEAD)

    def remote(src, dst, kind, kind_role, target):
        return pltpu.make_async_remote_copy(
            src_ref=src,
            dst_ref=dst,
            send_sem=send_sem.at[kind, kind_role],
            recv_sem=recv_sem.at[kind, kind_role],
            device_id={"ctx": target},
            device_id_type=MESH,
        )

    def push(src, dst, kind, kind_role, target):
        remote(src, dst, kind, kind_role, target).start()

    def landed(ref, kind, kind_role):
        remote(ref, ref, kind, kind_role, me).wait_recv()

    def left(ref, kind, kind_role):
        remote(ref, ref, kind, kind_role, me).wait_send()

    def worker(which, kind_role):
        return 2 * which + (kind_role + core) % 2

    def stage_peer(stride, size, turn):
        place = group // stride % size
        return group + ((place + turn) % size - place) * stride

    barrier = pltpu.get_barrier_semaphore()
    for turn in range(1, PEERS):
        pl.semaphore_signal(
            barrier, inc=1, device_id={"ctx": lax.rem(me + turn, PEERS)}, device_id_type=MESH
        )
    greeted = PEERS - 1
    for _, stride, size in stages:
        for turn in range(1, size):
            pl.semaphore_signal(
                barrier,
                inc=1,
                device_id={"dp": stage_peer(stride, size, turn)},
                device_id_type=MESH,
            )
            greeted += 1
    sums[...] = jnp.zeros(sums.shape, jnp.float32)
    for copy in staged[:4]:
        copy.wait()
    pl.semaphore_wait(barrier, greeted)

    @pl.when(role == 0)
    def _():
        box[:, 0, me] = own[:, 0, :, columns(head)]

    @pl.when(role == 1)
    def _():
        box[0, 1, me] = own[0, 1, :, columns(head)]
        box[1:, :, me] = own[1:, :, :, columns(head)]

    partner = group + 1 - 2 * core
    if STAGGER:

        @pl.when(core == 1)
        def _():
            pl.semaphore_wait(go_sem, 1)

    def each_worker(work):
        def step(turn, carry):
            which = lax.rem(head + turn, HEADS)

            @pl.when((turn > 0) | (role == 1))
            def _():
                work(which, 0, worker(which, 0))

            @pl.when((turn > 0) | (role == 0))
            def _():
                work(which, 1, worker(which, 1))

            return carry

        lax.fori_loop(0, HEADS, step, 0)

    def send_queries_keys(which, half, peer):
        cols = columns(which)
        push(own.at[0, half, :, cols], box.at[0, half, me], QUERY, half, peer)
        if half == 0:
            push(own.at[1, 0, :, cols], box.at[1, 0, me], KEY, 0, peer)
        else:
            push(own.at[1, :, :, cols], box.at[1, :, me], KEY, 1, peer)

    def send_values(which, half, peer):
        cols = columns(which)
        if half == 0:
            push(own.at[2, 0, :, cols], box.at[2, 0, me], VALUE, 0, peer)
        else:
            push(own.at[2, :, :, cols], box.at[2, :, me], VALUE, 1, peer)

    each_worker(send_queries_keys)
    each_worker(send_values)

    def by_role(work):
        for half in range(2):

            @pl.when(role == half)
            def _():
                work(half, HEADS - 1)

            @pl.when(role != half)
            def _():
                work(half, HEADS)

    def inputs_left():
        def wait(half, count):
            left(box.at[0, 0, :count], QUERY, half)
            if half == 0:
                left(box.at[1, 0, :count], KEY, 0)
                left(box.at[2, 0, :count], VALUE, 0)
            else:
                left(box.at[1, :, :count], KEY, 1)
                left(box.at[2, :, :count], VALUE, 1)

        by_role(wait)

    if STAGGER:

        @pl.when(core == 0)
        def _():
            inputs_left()
            pl.semaphore_signal(go_sem, inc=1, device_id={"dp": partner}, device_id_type=MESH)

    ends = []
    total = 0
    for user in range(lengths.shape[1]):
        total = total + lengths[0, user]
        ends.append(total)

    others = slice(0, PEERS - 1)

    @pl.when(role == 0)
    def _():
        landed(box.at[0, 0, others], QUERY, 0)
        landed(box.at[1, 0, others], KEY, 0)

    @pl.when(role == 1)
    def _():
        landed(box.at[0, 1, others], QUERY, 1)
        landed(box.at[1, :, others], KEY, 1)

    def rows_of(which, half, block):
        start = pl.multiple_of(block * PER_BLOCK, PER_BLOCK)
        return box[which, half, pl.ds(start, PER_BLOCK)].reshape(BLOCK, HEAD)

    def times(half, block, shape, axis):
        place = lax.broadcasted_iota(jnp.int32, shape, axis)
        chunk, inner = place // CHUNK, place % CHUNK
        shard = block * PER_BLOCK + chunk
        return jnp.where(half == 0, shard, 2 * PEERS - 1 - shard) * CHUNK + inner

    def key_block(step, part):
        early = (role == 0) | (part <= step)
        late_role = jnp.where(part <= step, 3 - step + part, part - 1)
        block = jnp.where(role == 0, min(part, STEPS - 1), late_role)
        return jnp.where(early, 0, 1), block

    def score_step(step, carry):
        q_block = rows_of(0, role, step)
        q_time = times(role, step, (BLOCK, 1), 0)
        first = jnp.zeros((BLOCK, 1), jnp.int32)
        for end in ends:
            first = jnp.where(q_time >= end, end, first)

        for part in range(PARTS):
            half, block = key_block(step, part)
            k_time = times(half, block, (1, BLOCK), 1)
            if part == STEPS:
                k_time = jnp.where(role == 0, 2 * HALF, k_time)
            raw = contract(q_block, rows_of(1, half, block), 1, 1)
            scores = raw * SCALE
            live = (k_time >= first) & (k_time <= q_time)
            sigmoid = 0.5 * jnp.tanh(raw * (0.5 * SCALE)) + 0.5
            silu = scores * sigmoid
            slope = sigmoid * SCALE + silu * (SCALE - SCALE * sigmoid)
            weights[step, part] = jnp.where(live, silu, 0.0).astype(jnp.bfloat16)
            slopes[step, part] = jnp.where(live, slope, 0.0)
        return carry

    lax.fori_loop(0, STEPS, score_step, 0)

    @pl.when(role == 0)
    def _():
        landed(box.at[2, 0, others], VALUE, 0)

    @pl.when(role == 1)
    def _():
        landed(box.at[2, :, others], VALUE, 1)

    def each_owner(step, work):
        for part in range(PER_BLOCK):
            shard = step * PER_BLOCK + part

            @pl.when(shard != me)
            def _():
                work(shard, False)

            @pl.when(shard == me)
            def _():
                work(shard, True)

    def deliver(src, dst, kind, target, here):
        if here:
            dst[...] = src[...]
        else:
            for half in range(2):

                @pl.when(role == half)
                def _():
                    push(src, dst, kind, half, target)

    def attend_step(step, carry):
        attended = jnp.zeros((BLOCK, HEAD), jnp.float32)
        for part in range(PARTS):
            half, block = key_block(step, part)
            attended = attended + contract(weights[step, part], rows_of(2, half, block), 1, 0)
        start = pl.multiple_of(step * PER_BLOCK, PER_BLOCK)
        att_out[pl.ds(start, PER_BLOCK)] = attended.astype(jnp.bfloat16).reshape(
            PER_BLOCK, CHUNK, HEAD
        )
        each_owner(
            step,
            lambda shard, here: deliver(
                att_out.at[shard], att_in.at[role, :, columns(head)], ATT, shard, here
            ),
        )
        return carry

    lax.fori_loop(0, STEPS, attend_step, 0)
    for copy in staged[4:]:
        copy.wait()
    gain_row = gain[...]
    by_role(lambda half, count: landed(att_in.at[half, :, : count * HEAD], ATT, half))

    def normalize(part, gain_sum):
        half, rows = part // 2, pl.ds(pl.multiple_of(part % 2 * 32, 32), 32)
        attended = att_in[half, rows, :].astype(jnp.float32)
        centered = attended - jnp.mean(attended, axis=1, keepdims=True)
        variance = jnp.mean(centered * centered, axis=1, keepdims=True)
        inverse = lax.rsqrt(variance + EPSILON)
        normed = centered * inverse
        gate = gates[half, rows, :].astype(jnp.float32)
        grad = cotangent[half, rows, :].astype(jnp.float32)
        scaled = gate * gain_row
        output[half, rows, :] = (normed * scaled).astype(jnp.bfloat16)
        gain_sum = gain_sum + jnp.sum(normed * grad * gate, axis=0, keepdims=True)
        grad = grad * scaled
        grad_out[half, rows, :] = (
            (
                grad
                - jnp.mean(grad, axis=1, keepdims=True)
                - normed * jnp.mean(grad * normed, axis=1, keepdims=True)
            )
            * inverse
        ).astype(jnp.bfloat16)
        return gain_sum

    gain_sum = lax.fori_loop(0, 4, normalize, jnp.zeros(gain_row.shape, jnp.float32))

    grad_in[me] = grad_out[role, :, columns(head)]
    each_worker(
        lambda which, half, peer: push(
            grad_out.at[half, :, columns(which)], grad_in.at[me], GRAD, half, peer
        )
    )

    def gain_copy(slot, stage, target):
        return pltpu.make_async_remote_copy(
            src_ref=slot,
            dst_ref=slot,
            send_sem=gain_send_sem.at[stage],
            recv_sem=gain_recv_sem.at[stage],
            device_id={"dp": target},
            device_id_type=MESH,
        )

    for which in range(HEADS):
        gain_slots[me, which : which + 1, :] = gain_sum[:, which * HEAD : (which + 1) * HEAD]

    def send_gain(turn, carry):
        push(gain_slots.at[me], gain_slots.at[me], GAIN, 0, lax.rem(me + turn, PEERS))
        return carry

    lax.fori_loop(1, PEERS, send_gain, 0)

    def gain_send(stage, total):
        slot, stride, size = stages[stage]
        mine = slot + group // stride % size
        gain_slots[mine] = total
        for turn in range(1, size):
            gain_copy(gain_slots.at[mine], stage, stage_peer(stride, size, turn)).start()

    def gain_stage_sum(stage):
        slot, stride, size = stages[stage]
        gain_copy(gain_slots.at[slot : slot + size - 1], stage, group).wait_recv()
        return jnp.sum(gain_slots[slot : slot + size], axis=0)

    for half in range(2):

        @pl.when(role == half)
        def _():
            landed(grad_in.at[others], GRAD, half)

    def flip(matrix):
        return matrix.astype(jnp.float32).T.astype(jnp.bfloat16)

    def finish(half, block):
        place = pl.ds(pl.multiple_of(half * HALF + block * BLOCK, BLOCK), BLOCK)
        start = pl.multiple_of(block * PER_BLOCK, PER_BLOCK)
        for index in range(2):
            out_box[1 + index, half, pl.ds(start, PER_BLOCK)] = (
                sums[index, :, place].T.astype(jnp.bfloat16).reshape(PER_BLOCK, CHUNK, HEAD)
            )

    def backward_step(turn, carry):
        step = jnp.where(role == 0, STEPS - 1 - turn, turn)
        start = pl.multiple_of(step * PER_BLOCK, PER_BLOCK)
        grad = grad_in[pl.ds(start, PER_BLOCK)].reshape(BLOCK, HEAD)
        grad_flipped = flip(grad)
        q_flipped = flip(rows_of(0, role, step))
        dq = jnp.zeros((BLOCK, HEAD), jnp.float32)
        for part in range(PARTS):
            half, block = key_block(step, part)
            place = pl.ds(pl.multiple_of(half * HALF + block * BLOCK, BLOCK), BLOCK)
            grad_weights = contract(grad, rows_of(2, half, block), 1, 1)
            grad_scores = (grad_weights * slopes[step, part]).astype(jnp.bfloat16)
            sums[0, :, place] += contract(q_flipped, grad_scores, 1, 0)
            sums[1, :, place] += contract(grad_flipped, weights[step, part], 1, 0)
            dq = dq + contract(grad_scores, rows_of(1, half, block), 1, 0)
        out_box[0, role, pl.ds(start, PER_BLOCK)] = dq.astype(jnp.bfloat16).reshape(
            PER_BLOCK, CHUNK, HEAD
        )
        finish(role, step)

        def send(shard, here):
            for half in range(2):

                @pl.when(role == half)
                def _():
                    back = back_early if half == 0 else back_late.at[:, 1]
                    src, dst = out_box.at[:, half, shard], back.at[:, :, columns(head)]
                    if here:
                        dst[...] = src[...]
                    else:
                        push(src, dst, BACK, half, shard)

        each_owner(step, send)
        return carry

    lax.fori_loop(0, STEPS, backward_step, 0)

    @pl.when(role == 1)
    def _():
        def finish_early(block, carry):
            finish(0, block)

            def send(shard, here):
                src, dst = out_box.at[1:, 0, shard], back_late.at[1:, 0, :, columns(head)]
                if here:
                    dst[...] = src[...]
                else:
                    push(src, dst, BACK_E, 0, shard)

            each_owner(block, send)
            return carry

        lax.fori_loop(0, STEPS, finish_early, 0)

    landed(gain_slots.at[others], GAIN, 0)
    total = jnp.sum(gain_slots[:PEERS], axis=0)
    for stage in range(len(stages)):
        gain_send(stage, total)
        total = gain_stage_sum(stage)
    gain_total[...] = total

    def wait_back(half, count):
        cols = slice(0, count * HEAD)
        if half == 0:
            landed(back_early.at[:, :, cols], BACK, 0)
        else:
            landed(back_late.at[:, 1, :, cols], BACK, 1)
            landed(back_late.at[1:, 0, :, cols], BACK_E, 0)

    by_role(wait_back)
    grad_queries[0] = back_early[0]
    grad_queries[1] = back_late[0, 1]
    for index, result in ((1, grad_keys), (2, grad_values)):
        result[0] = (
            back_early[index].astype(jnp.float32) + back_late[index, 0].astype(jnp.float32)
        ).astype(jnp.bfloat16)
        result[1] = back_late[index, 1]

    if STAGGER:

        @pl.when(core == 1)
        def _():
            inputs_left()

    else:
        inputs_left()
    for half in range(2):

        @pl.when(role == half)
        def _():
            left(att_out.at[others], ATT, half)
            left(out_box.at[:, 0, others], BACK, half)
            if half == 1:
                left(out_box.at[1:, 0, others], BACK_E, 0)

    by_role(lambda half, count: left(grad_in.at[:count], GRAD, half))
    left(gain_slots.at[others], GAIN, 0)
    for stage, (slot, _, size) in enumerate(stages):
        gain_copy(gain_slots.at[slot : slot + size - 1], stage, group).wait_send()


def hand_over(*refs):
    count = (len(refs) - 1) // 2
    copies = [
        pltpu.make_async_copy(src, dst, refs[-1].at[index])
        for index, (src, dst) in enumerate(zip(refs[:count], refs[count : 2 * count]))
    ]
    for copy in copies:
        copy.start()
    for copy in copies:
        copy.wait()


def body(queries, key_vectors, value_vectors, gate_values, cotangent, norm_gain, lengths):
    row_count, width = queries.shape
    groups = lax.axis_size("dp")
    _, slots = gain_stages(groups)
    halves = (2, CHUNK, width)
    wide = jax.ShapeDtypeStruct(halves, jnp.bfloat16)
    vmem = pl.BlockSpec(memory_space=pltpu.VMEM)
    hbm = pl.BlockSpec(memory_space=pltpu.HBM)

    def kernel(*refs):
        attention_kernel(groups, *refs)

    shapes = (wide, wide, wide, wide, jax.ShapeDtypeStruct((HEADS, HEAD), jnp.float32))
    results = pl.pallas_call(
        kernel,
        out_shape=shapes,
        in_specs=[hbm] * 7,
        out_specs=(vmem,) * 5,
        scratch_shapes=[
            pltpu.SMEM(lengths.shape, jnp.int32),
            pltpu.VMEM((3,) + halves, jnp.bfloat16),
            pltpu.VMEM(halves, jnp.bfloat16),
            pltpu.VMEM(halves, jnp.bfloat16),
            pltpu.VMEM((1, width), jnp.float32),
            pltpu.VMEM((3, 2, PEERS, CHUNK, HEAD), jnp.bfloat16),
            pltpu.VMEM((STEPS, PARTS, BLOCK, BLOCK), jnp.bfloat16),
            pltpu.VMEM((STEPS, PARTS, BLOCK, BLOCK), jnp.float32),
            pltpu.VMEM((PEERS, CHUNK, HEAD), jnp.bfloat16),
            pltpu.VMEM(halves, jnp.bfloat16),
            pltpu.VMEM(halves, jnp.bfloat16),
            pltpu.VMEM((PEERS, CHUNK, HEAD), jnp.bfloat16),
            pltpu.VMEM((2, HEAD, 2 * HALF), jnp.float32),
            pltpu.VMEM((3, 2, PEERS, CHUNK, HEAD), jnp.bfloat16),
            pltpu.VMEM((3, CHUNK, width), jnp.bfloat16),
            pltpu.VMEM((3, 2, CHUNK, width), jnp.bfloat16),
            pltpu.VMEM((slots, HEADS, HEAD), jnp.float32),
            pltpu.SemaphoreType.DMA((7,)),
            pltpu.SemaphoreType.DMA((KINDS, 2)),
            pltpu.SemaphoreType.DMA((KINDS, 2)),
            pltpu.SemaphoreType.DMA((8,)),
            pltpu.SemaphoreType.DMA((8,)),
            pltpu.SemaphoreType.REGULAR,
        ],
        compiler_params=pltpu.CompilerParams(
            collective_id=0, has_side_effects=True, vmem_limit_bytes=60 * 2**20
        ),
    )(
        lengths,
        *(
            array.reshape(halves)
            for array in (queries, key_vectors, value_vectors, gate_values, cotangent)
        ),
        norm_gain.reshape(1, width),
    )
    *grads, gain_total = pl.pallas_call(
        hand_over,
        out_shape=shapes,
        in_specs=[vmem] * 5,
        out_specs=(hbm,) * 5,
        scratch_shapes=[pltpu.SemaphoreType.DMA((5,))],
    )(*results)
    return *(array.reshape(row_count, width) for array in grads), gain_total.reshape(width)


def solution(mesh):
    rows = P(("dp", "ctx"), None)
    return jax.shard_map(
        body,
        mesh=mesh,
        in_specs=(rows,) * 5 + (P(), P("dp", None)),
        out_specs=(rows,) * 4 + (P(),),
        check_vma=False,
    )
```

```python
import math

import jax
import jax.numpy as jnp
from jax import lax
from jax.experimental import pallas as pl
from jax.experimental.pallas import tpu as pltpu
from jax.sharding import PartitionSpec as P

HEAD = 128
EPSILON = 1e-05
PEERS = 16
HEADS = 8
CHUNK = 64
HALF = PEERS * CHUNK
BLOCK = 256
PER_BLOCK = BLOCK // CHUNK
STEPS = HALF // BLOCK
PARTS = STEPS + 1
SCALE = 1.0 / math.sqrt(HEAD)

QUERY, KEY, VALUE, ATT, GRAD, BACK, BACK_E, GAIN, GAIN_CORE, GAIN_LAYER = range(10)
KINDS = 10
MESH = pl.DeviceIdType.MESH


def contract(left, right, left_axis, right_axis):
    return lax.dot_general(
        left, right, (((left_axis,), (right_axis,)), ((), ())), preferred_element_type=jnp.float32
    )


def attention_kernel(
    groups,
    lengths_hbm,
    queries_hbm,
    keys_hbm,
    values_hbm,
    gates_hbm,
    cotangent_hbm,
    gain_hbm,
    output,
    grad_queries,
    grad_keys,
    grad_values,
    gain_total,
    lengths,
    own,
    gates,
    cotangent,
    gain,
    box,
    weights,
    slopes,
    att_out,
    att_in,
    grad_out,
    grad_in,
    sums,
    out_box,
    back_early,
    back_late,
    gain_slots,
    local_sem,
    send_sem,
    recv_sem,
    word_sem,
):
    me = lax.axis_index("ctx")
    group = lax.axis_index("dp")
    core = group % 2
    head = me // 2
    role = (me + core) % 2
    place_z, layers = group // 2, groups // 2
    partner = group + 1 - 2 * core

    staged = [
        pltpu.make_async_copy(src, dst, local_sem.at[index])
        for index, (src, dst) in enumerate(
            (
                (queries_hbm, own.at[0]),
                (keys_hbm, own.at[1]),
                (values_hbm, own.at[2]),
                (lengths_hbm, lengths),
                (gates_hbm, gates),
                (cotangent_hbm, cotangent),
                (gain_hbm, gain),
            )
        )
    ]
    for copy in staged:
        copy.start()

    def columns(which):
        return pl.ds(pl.multiple_of(which * HEAD, HEAD), HEAD)

    def remote(src, dst, kind, kind_role, target):
        return pltpu.make_async_remote_copy(
            src_ref=src,
            dst_ref=dst,
            send_sem=send_sem.at[kind, kind_role],
            recv_sem=recv_sem.at[kind, kind_role],
            device_id={"ctx": target},
            device_id_type=MESH,
        )

    def push(src, dst, kind, kind_role, target):
        remote(src, dst, kind, kind_role, target).start()

    def landed(ref, kind, kind_role):
        remote(ref, ref, kind, kind_role, me).wait_recv()

    def left(ref, kind, kind_role):
        remote(ref, ref, kind, kind_role, me).wait_send()

    def worker(which, kind_role):
        return 2 * which + (kind_role + core) % 2

    def layer(distance):
        return 2 * lax.rem(place_z + distance + layers, layers) + core

    barrier = pltpu.get_barrier_semaphore()
    for turn in range(1, PEERS):
        pl.semaphore_signal(
            barrier, inc=1, device_id={"ctx": lax.rem(me + turn, PEERS)}, device_id_type=MESH
        )
    neighbours = [partner] + ([layer(1), layer(-1)] if layers > 1 else [])
    for peer in neighbours:
        pl.semaphore_signal(barrier, inc=1, device_id={"dp": peer}, device_id_type=MESH)
    sums[...] = jnp.zeros(sums.shape, jnp.float32)
    for copy in staged[:4]:
        copy.wait()
    pl.semaphore_wait(barrier, PEERS - 1 + len(neighbours))

    @pl.when(role == 0)
    def _():
        box[:, 0, me] = own[:, 0, :, columns(head)]

    @pl.when(role == 1)
    def _():
        box[0, 1, me] = own[0, 1, :, columns(head)]
        box[1:, :, me] = own[1:, :, :, columns(head)]

    rounds = [1 << index for index in range(8) if 1 << index < layers // 2 + layers % 2]

    def pass_word(index):
        if index < len(rounds):
            for distance in (rounds[index], -rounds[index]):
                pl.semaphore_signal(
                    word_sem.at[index], inc=1, device_id={"dp": layer(distance)}, device_id_type=MESH
                )

    def hear_word(index):
        if index < len(rounds):
            pl.semaphore_wait(word_sem.at[index], 2)

    def each_worker(work):
        def step(turn, carry):
            which = lax.rem(head + turn, HEADS)

            @pl.when((turn > 0) | (role == 1))
            def _():
                work(which, 0, worker(which, 0))

            @pl.when((turn > 0) | (role == 0))
            def _():
                work(which, 1, worker(which, 1))

            return carry

        lax.fori_loop(0, HEADS, step, 0)

    def send_queries_keys(which, half, peer):
        cols = columns(which)
        push(own.at[0, half, :, cols], box.at[0, half, me], QUERY, half, peer)
        if half == 0:
            push(own.at[1, 0, :, cols], box.at[1, 0, me], KEY, 0, peer)
        else:
            push(own.at[1, :, :, cols], box.at[1, :, me], KEY, 1, peer)

    def send_values(which, half, peer):
        cols = columns(which)
        if half == 0:
            push(own.at[2, 0, :, cols], box.at[2, 0, me], VALUE, 0, peer)
        else:
            push(own.at[2, :, :, cols], box.at[2, :, me], VALUE, 1, peer)

    each_worker(send_queries_keys)
    each_worker(send_values)

    def by_role(work):
        for half in range(2):

            @pl.when(role == half)
            def _():
                work(half, HEADS - 1)

            @pl.when(role != half)
            def _():
                work(half, HEADS)

    def inputs_left():
        def wait(half, count):
            left(box.at[0, 0, :count], QUERY, half)
            if half == 0:
                left(box.at[1, 0, :count], KEY, 0)
                left(box.at[2, 0, :count], VALUE, 0)
            else:
                left(box.at[1, :, :count], KEY, 1)
                left(box.at[2, :, :count], VALUE, 1)

        by_role(wait)

    pass_word(0)

    ends = []
    total = 0
    for user in range(lengths.shape[1]):
        total = total + lengths[0, user]
        ends.append(total)

    others = slice(0, PEERS - 1)

    @pl.when(role == 0)
    def _():
        landed(box.at[0, 0, others], QUERY, 0)
        landed(box.at[1, 0, others], KEY, 0)

    @pl.when(role == 1)
    def _():
        landed(box.at[0, 1, others], QUERY, 1)
        landed(box.at[1, :, others], KEY, 1)

    def rows_of(which, half, block):
        start = pl.multiple_of(block * PER_BLOCK, PER_BLOCK)
        return box[which, half, pl.ds(start, PER_BLOCK)].reshape(BLOCK, HEAD)

    def times(half, block, shape, axis):
        place = lax.broadcasted_iota(jnp.int32, shape, axis)
        chunk, inner = place // CHUNK, place % CHUNK
        shard = block * PER_BLOCK + chunk
        return jnp.where(half == 0, shard, 2 * PEERS - 1 - shard) * CHUNK + inner

    def key_block(step, part):
        early = (role == 0) | (part <= step)
        late_role = jnp.where(part <= step, 3 - step + part, part - 1)
        block = jnp.where(role == 0, min(part, STEPS - 1), late_role)
        return jnp.where(early, 0, 1), block

    def score_step(step, carry):
        q_block = rows_of(0, role, step)
        q_time = times(role, step, (BLOCK, 1), 0)
        first = jnp.zeros((BLOCK, 1), jnp.int32)
        for end in ends:
            first = jnp.where(q_time >= end, end, first)

        for part in range(PARTS):
            half, block = key_block(step, part)
            k_time = times(half, block, (1, BLOCK), 1)
            if part == STEPS:
                k_time = jnp.where(role == 0, 2 * HALF, k_time)
            raw = contract(q_block, rows_of(1, half, block), 1, 1)
            scores = raw * SCALE
            live = (k_time >= first) & (k_time <= q_time)
            sigmoid = 0.5 * jnp.tanh(raw * (0.5 * SCALE)) + 0.5
            silu = scores * sigmoid
            slope = sigmoid * SCALE + silu * (SCALE - SCALE * sigmoid)
            weights[step, part] = jnp.where(live, silu, 0.0).astype(jnp.bfloat16)
            slopes[step, part] = jnp.where(live, slope, 0.0)
        return carry

    lax.fori_loop(0, STEPS, score_step, 0)
    hear_word(0)
    pass_word(1)

    @pl.when(role == 0)
    def _():
        landed(box.at[2, 0, others], VALUE, 0)

    @pl.when(role == 1)
    def _():
        landed(box.at[2, :, others], VALUE, 1)

    def each_owner(step, work):
        for part in range(PER_BLOCK):
            shard = step * PER_BLOCK + part

            @pl.when(shard != me)
            def _():
                work(shard, False)

            @pl.when(shard == me)
            def _():
                work(shard, True)

    def deliver(src, dst, kind, target, here):
        if here:
            dst[...] = src[...]
        else:
            for half in range(2):

                @pl.when(role == half)
                def _():
                    push(src, dst, kind, half, target)

    def attend_step(step, carry):
        attended = jnp.zeros((BLOCK, HEAD), jnp.float32)
        for part in range(PARTS):
            half, block = key_block(step, part)
            attended = attended + contract(weights[step, part], rows_of(2, half, block), 1, 0)
        start = pl.multiple_of(step * PER_BLOCK, PER_BLOCK)
        att_out[pl.ds(start, PER_BLOCK)] = attended.astype(jnp.bfloat16).reshape(
            PER_BLOCK, CHUNK, HEAD
        )
        each_owner(
            step,
            lambda shard, here: deliver(
                att_out.at[shard], att_in.at[role, :, columns(head)], ATT, shard, here
            ),
        )
        return carry

    lax.fori_loop(0, STEPS, attend_step, 0)
    hear_word(1)
    pass_word(2)
    for copy in staged[4:]:
        copy.wait()
    gain_row = gain[...]
    by_role(lambda half, count: landed(att_in.at[half, :, : count * HEAD], ATT, half))

    def normalize(part, gain_sum):
        half, rows = part // 2, pl.ds(pl.multiple_of(part % 2 * 32, 32), 32)
        attended = att_in[half, rows, :].astype(jnp.float32)
        centered = attended - jnp.mean(attended, axis=1, keepdims=True)
        variance = jnp.mean(centered * centered, axis=1, keepdims=True)
        inverse = lax.rsqrt(variance + EPSILON)
        normed = centered * inverse
        gate = gates[half, rows, :].astype(jnp.float32)
        grad = cotangent[half, rows, :].astype(jnp.float32)
        scaled = gate * gain_row
        output[half, rows, :] = (normed * scaled).astype(jnp.bfloat16)
        gain_sum = gain_sum + jnp.sum(normed * grad * gate, axis=0, keepdims=True)
        grad = grad * scaled
        grad_out[half, rows, :] = (
            (
                grad
                - jnp.mean(grad, axis=1, keepdims=True)
                - normed * jnp.mean(grad * normed, axis=1, keepdims=True)
            )
            * inverse
        ).astype(jnp.bfloat16)
        return gain_sum

    gain_sum = lax.fori_loop(0, 4, normalize, jnp.zeros(gain_row.shape, jnp.float32))

    grad_in[me] = grad_out[role, :, columns(head)]
    each_worker(
        lambda which, half, peer: push(
            grad_out.at[half, :, columns(which)], grad_in.at[me], GRAD, half, peer
        )
    )

    both, along = PEERS, PEERS + 2

    def gain_copy(slots, kind, target):
        return pltpu.make_async_remote_copy(
            src_ref=slots,
            dst_ref=slots,
            send_sem=send_sem.at[kind, 0],
            recv_sem=recv_sem.at[kind, 0],
            device_id={"dp": target},
            device_id_type=MESH,
        )

    for which in range(HEADS):
        gain_slots[me, which : which + 1, :] = gain_sum[:, which * HEAD : (which + 1) * HEAD]

    def send_gain(turn, carry):
        push(gain_slots.at[me], gain_slots.at[me], GAIN, 0, lax.rem(me + turn, PEERS))
        return carry

    lax.fori_loop(1, PEERS, send_gain, 0)

    def gain_over_cores():
        landed(gain_slots.at[others], GAIN, 0)
        gain_slots[both + core] = jnp.sum(gain_slots[:PEERS], axis=0)
        gain_copy(gain_slots.at[both + core], GAIN_CORE, partner).start()

    def gain_over_layers():
        gain_copy(gain_slots.at[both], GAIN_CORE, partner).wait_recv()
        mine = along + place_z
        gain_slots[mine] = gain_slots[both] + gain_slots[both + 1]

        def send(distance, carry):
            gain_copy(gain_slots.at[mine], GAIN_LAYER, layer(distance)).start()
            return carry

        lax.fori_loop(1, layers, send, 0)

    hear_word(2)
    for half in range(2):

        @pl.when(role == half)
        def _():
            landed(grad_in.at[others], GRAD, half)

    def flip(matrix):
        return matrix.astype(jnp.float32).T.astype(jnp.bfloat16)

    def finish(half, block):
        place = pl.ds(pl.multiple_of(half * HALF + block * BLOCK, BLOCK), BLOCK)
        start = pl.multiple_of(block * PER_BLOCK, PER_BLOCK)
        for index in range(2):
            out_box[1 + index, half, pl.ds(start, PER_BLOCK)] = (
                sums[index, :, place].T.astype(jnp.bfloat16).reshape(PER_BLOCK, CHUNK, HEAD)
            )

    gain_over_cores()

    def backward_step(turn, carry):
        pl.when(turn == 2)(gain_over_layers)
        step = jnp.where(role == 0, STEPS - 1 - turn, turn)
        start = pl.multiple_of(step * PER_BLOCK, PER_BLOCK)
        grad = grad_in[pl.ds(start, PER_BLOCK)].reshape(BLOCK, HEAD)
        grad_flipped = flip(grad)
        q_flipped = flip(rows_of(0, role, step))
        dq = jnp.zeros((BLOCK, HEAD), jnp.float32)
        for part in range(PARTS):
            half, block = key_block(step, part)
            place = pl.ds(pl.multiple_of(half * HALF + block * BLOCK, BLOCK), BLOCK)
            grad_weights = contract(grad, rows_of(2, half, block), 1, 1)
            grad_scores = (grad_weights * slopes[step, part]).astype(jnp.bfloat16)
            sums[0, :, place] += contract(q_flipped, grad_scores, 1, 0)
            sums[1, :, place] += contract(grad_flipped, weights[step, part], 1, 0)
            dq = dq + contract(grad_scores, rows_of(1, half, block), 1, 0)
        out_box[0, role, pl.ds(start, PER_BLOCK)] = dq.astype(jnp.bfloat16).reshape(
            PER_BLOCK, CHUNK, HEAD
        )
        finish(role, step)

        def send(shard, here):
            for half in range(2):

                @pl.when(role == half)
                def _():
                    back = back_early if half == 0 else back_late.at[:, 1]
                    src, dst = out_box.at[:, half, shard], back.at[:, :, columns(head)]
                    if here:
                        dst[...] = src[...]
                    else:
                        push(src, dst, BACK, half, shard)

        each_owner(step, send)
        return carry

    lax.fori_loop(0, STEPS, backward_step, 0)

    @pl.when(role == 1)
    def _():
        def finish_early(block, carry):
            finish(0, block)

            def send(shard, here):
                src, dst = out_box.at[1:, 0, shard], back_late.at[1:, 0, :, columns(head)]
                if here:
                    dst[...] = src[...]
                else:
                    push(src, dst, BACK_E, 0, shard)

            each_owner(block, send)
            return carry

        lax.fori_loop(0, STEPS, finish_early, 0)

    def wait_back(half, count):
        cols = slice(0, count * HEAD)
        if half == 0:
            landed(back_early.at[:, :, cols], BACK, 0)
        else:
            landed(back_late.at[:, 1, :, cols], BACK, 1)
            landed(back_late.at[1:, 0, :, cols], BACK_E, 0)

    by_role(wait_back)
    if layers > 1:
        gain_copy(gain_slots.at[along : along + layers - 1], GAIN_LAYER, partner).wait_recv()
    gain_total[...] = jnp.sum(gain_slots[along : along + layers], axis=0)
    grad_queries[0] = back_early[0]
    grad_queries[1] = back_late[0, 1]
    for index, result in ((1, grad_keys), (2, grad_values)):
        result[0] = (
            back_early[index].astype(jnp.float32) + back_late[index, 0].astype(jnp.float32)
        ).astype(jnp.bfloat16)
        result[1] = back_late[index, 1]

    inputs_left()
    for half in range(2):

        @pl.when(role == half)
        def _():
            left(att_out.at[others], ATT, half)
            left(out_box.at[:, 0, others], BACK, half)
            if half == 1:
                left(out_box.at[1:, 0, others], BACK_E, 0)

    by_role(lambda half, count: left(grad_in.at[:count], GRAD, half))
    left(gain_slots.at[others], GAIN, 0)
    gain_copy(gain_slots.at[both], GAIN_CORE, partner).wait_send()
    if layers > 1:
        gain_copy(gain_slots.at[along : along + layers - 1], GAIN_LAYER, partner).wait_send()


def hand_over(*refs):
    count = (len(refs) - 1) // 2
    copies = [
        pltpu.make_async_copy(src, dst, refs[-1].at[index])
        for index, (src, dst) in enumerate(zip(refs[:count], refs[count : 2 * count]))
    ]
    for copy in copies:
        copy.start()
    for copy in copies:
        copy.wait()


def body(queries, key_vectors, value_vectors, gate_values, cotangent, norm_gain, lengths):
    row_count, width = queries.shape
    groups = lax.axis_size("dp")
    halves = (2, CHUNK, width)
    wide = jax.ShapeDtypeStruct(halves, jnp.bfloat16)
    vmem = pl.BlockSpec(memory_space=pltpu.VMEM)
    hbm = pl.BlockSpec(memory_space=pltpu.HBM)

    def kernel(*refs):
        attention_kernel(groups, *refs)

    shapes = (wide, wide, wide, wide, jax.ShapeDtypeStruct((HEADS, HEAD), jnp.float32))
    results = pl.pallas_call(
        kernel,
        out_shape=shapes,
        in_specs=[hbm] * 7,
        out_specs=(vmem,) * 5,
        scratch_shapes=[
            pltpu.SMEM(lengths.shape, jnp.int32),
            pltpu.VMEM((3,) + halves, jnp.bfloat16),
            pltpu.VMEM(halves, jnp.bfloat16),
            pltpu.VMEM(halves, jnp.bfloat16),
            pltpu.VMEM((1, width), jnp.float32),
            pltpu.VMEM((3, 2, PEERS, CHUNK, HEAD), jnp.bfloat16),
            pltpu.VMEM((STEPS, PARTS, BLOCK, BLOCK), jnp.bfloat16),
            pltpu.VMEM((STEPS, PARTS, BLOCK, BLOCK), jnp.float32),
            pltpu.VMEM((PEERS, CHUNK, HEAD), jnp.bfloat16),
            pltpu.VMEM(halves, jnp.bfloat16),
            pltpu.VMEM(halves, jnp.bfloat16),
            pltpu.VMEM((PEERS, CHUNK, HEAD), jnp.bfloat16),
            pltpu.VMEM((2, HEAD, 2 * HALF), jnp.float32),
            pltpu.VMEM((3, 2, PEERS, CHUNK, HEAD), jnp.bfloat16),
            pltpu.VMEM((3, CHUNK, width), jnp.bfloat16),
            pltpu.VMEM((3, 2, CHUNK, width), jnp.bfloat16),
            pltpu.VMEM((PEERS + 2 + groups // 2, HEADS, HEAD), jnp.float32),
            pltpu.SemaphoreType.DMA((7,)),
            pltpu.SemaphoreType.DMA((KINDS, 2)),
            pltpu.SemaphoreType.DMA((KINDS, 2)),
            pltpu.SemaphoreType.REGULAR((8,)),
        ],
        compiler_params=pltpu.CompilerParams(
            collective_id=0, has_side_effects=True, vmem_limit_bytes=60 * 2**20
        ),
    )(
        lengths,
        *(
            array.reshape(halves)
            for array in (queries, key_vectors, value_vectors, gate_values, cotangent)
        ),
        norm_gain.reshape(1, width),
    )
    *grads, gain_total = pl.pallas_call(
        hand_over,
        out_shape=shapes,
        in_specs=[vmem] * 5,
        out_specs=(hbm,) * 5,
        scratch_shapes=[pltpu.SemaphoreType.DMA((5,))],
    )(*results)
    return *(array.reshape(row_count, width) for array in grads), gain_total.reshape(width)


def solution(mesh):
    rows = P(("dp", "ctx"), None)
    return jax.shard_map(
        body,
        mesh=mesh,
        in_specs=(rows,) * 5 + (P(), P("dp", None)),
        out_specs=(rows,) * 4 + (P(),),
        check_vma=False,
    )
```

```python
import math

import jax
import jax.numpy as jnp
from jax import lax
from jax.experimental import pallas as pl
from jax.experimental.pallas import tpu as pltpu
from jax.sharding import PartitionSpec as P

HEAD = 128
EPSILON = 1e-05
PEERS = 16
HEADS = 8
CHUNK = 64
HALF = PEERS * CHUNK
BLOCK = 256
PER_BLOCK = BLOCK // CHUNK
BLOCKS = HALF // BLOCK
PARTS = BLOCKS + 1
EARLY_STEPS = BLOCKS // 2
STEPS = EARLY_STEPS + BLOCKS
SCALE = 1.0 / math.sqrt(HEAD)

QUERY_KEY, VALUE, ATT, GRAD, DQ, DKV, GAIN, GAIN_CORE, GAIN_LAYER, GAIN_TOTAL = range(10)
KINDS = 10
MESH = pl.DeviceIdType.MESH


def contract(left, right, left_axis, right_axis):
    return lax.dot_general(
        left, right, (((left_axis,), (right_axis,)), ((), ())), preferred_element_type=jnp.float32
    )


def attention_kernel(
    groups,
    lengths_hbm,
    queries_hbm,
    keys_hbm,
    values_hbm,
    gates_hbm,
    cotangent_hbm,
    gain_hbm,
    output_hbm,
    grad_queries_hbm,
    grad_keys_hbm,
    grad_values_hbm,
    gain_total_hbm,
    lengths,
    own,
    gates,
    cotangent,
    gain,
    box,
    bounds,
    weights,
    slopes,
    att_sum,
    att_out,
    att_in,
    output,
    grad_out,
    grad_in,
    q_flipped,
    grad_flipped,
    dq_sum,
    sums,
    out_box,
    back,
    gain_slots,
    gain_total,
    local_sem,
    out_sem,
    send_sem,
    recv_sem,
    word_sem,
):
    me = lax.axis_index("ctx")
    group = lax.axis_index("dp")
    core = group % 2
    head = me // 2
    works = me % 2 == core
    place_z, layers = group // 2, groups // 2
    mate = me + 1 - 2 * (me % 2)
    partner = group + 1 - 2 * core
    others = slice(0, PEERS - 1)

    staged = [
        pltpu.make_async_copy(src, dst, local_sem.at[index])
        for index, (src, dst) in enumerate(
            (
                (queries_hbm, own.at[0]),
                (keys_hbm, own.at[1]),
                (values_hbm, own.at[2]),
                (lengths_hbm, lengths),
                (gates_hbm, gates),
                (cotangent_hbm, cotangent),
                (gain_hbm, gain),
            )
        )
    ]
    for copy in staged:
        copy.start()

    def columns(which):
        return pl.ds(pl.multiple_of(which * HEAD, HEAD), HEAD)

    def remote(src, dst, kind, half, target):
        return pltpu.make_async_remote_copy(
            src_ref=src,
            dst_ref=dst,
            send_sem=send_sem.at[kind, half],
            recv_sem=recv_sem.at[kind, half],
            device_id={"ctx": target},
            device_id_type=MESH,
        )

    def push(src, dst, kind, half, target):
        remote(src, dst, kind, half, target).start()

    def landed(ref, kind, half=0):
        remote(ref, ref, kind, half, me).wait_recv()

    def left(ref, kind, half=0):
        remote(ref, ref, kind, half, me).wait_send()

    def layer(distance):
        return 2 * lax.rem(place_z + distance + layers, layers) + core

    barrier = pltpu.get_barrier_semaphore()
    for turn in range(1, PEERS):
        pl.semaphore_signal(
            barrier, inc=1, device_id={"ctx": lax.rem(me + turn, PEERS)}, device_id_type=MESH
        )
    near = [{"dp": partner, "ctx": mate}]
    if layers > 1:
        near += [{"dp": layer(1)}, {"dp": layer(-1)}]

    @pl.when(jnp.logical_not(works))
    def _():
        for peer in near:
            pl.semaphore_signal(barrier, inc=1, device_id=peer, device_id_type=MESH)

    for copy in staged[:4]:
        copy.wait()

    @pl.when(works)
    def _():
        pl.semaphore_wait(barrier, PEERS - 1)

    @pl.when(jnp.logical_not(works))
    def _():
        pl.semaphore_wait(barrier, PEERS - 1 + len(near))

    rounds = [1 << index for index in range(8) if 1 << index < layers // 2 + layers % 2]

    def pass_words():
        for index, reach in enumerate(rounds):
            for distance in (reach, -reach):
                pl.semaphore_signal(
                    word_sem.at[index], inc=1, device_id={"dp": layer(distance)}, device_id_type=MESH
                )
            pl.semaphore_wait(word_sem.at[index], 2)

    def each_worker(work):
        def step(turn, carry):
            which = lax.rem(head + turn, HEADS)
            work(which, 2 * which + core)
            return carry

        lax.fori_loop(jnp.where(works, 1, 0), HEADS, step, 0)

    def by_count(work):
        @pl.when(works)
        def _():
            work(HEADS - 1)

        @pl.when(jnp.logical_not(works))
        def _():
            work(HEADS)

    each_worker(
        lambda which, peer: push(
            own.at[:2, :, :, columns(which)], box.at[:2, :, me], QUERY_KEY, 0, peer
        )
    )

    @pl.when(works)
    def _():
        box[:, :, me] = own[:, :, :, columns(head)]

    by_count(lambda count: left(box.at[:2, :, :count], QUERY_KEY))
    each_worker(
        lambda which, peer: push(own.at[2, :, :, columns(which)], box.at[2, :, me], VALUE, 0, peer)
    )
    pl.when(jnp.logical_not(works))(pass_words)

    def times(half, block, shape, axis):
        place = lax.broadcasted_iota(jnp.int32, shape, axis)
        chunk, inner = place // CHUNK, place % CHUNK
        shard = block * PER_BLOCK + chunk
        return jnp.where(half == 0, shard, 2 * PEERS - 1 - shard) * CHUNK + inner

    def rows_of(which, half, block):
        start = pl.multiple_of(block * PER_BLOCK, PER_BLOCK)
        return box[which, half, pl.ds(start, PER_BLOCK)].reshape(BLOCK, HEAD)

    def chunks(block):
        return pl.ds(pl.multiple_of(block * PER_BLOCK, PER_BLOCK), PER_BLOCK)

    def place_of(half, block):
        return pl.ds(pl.multiple_of(half * HALF + block * BLOCK, BLOCK), BLOCK)

    def pair(step, part):
        early = step < EARLY_STEPS
        short = part <= step
        late_block = step - EARLY_STEPS
        reaches_back = part <= late_block
        q_half = jnp.where(early, 0, 1)
        q_block = jnp.where(early, jnp.where(short, step, BLOCKS - 1 - step), late_block)
        k_half = jnp.where(early | reaches_back, 0, 1)
        k_block = jnp.where(
            early,
            jnp.where(short, part, part - step - 1),
            jnp.where(reaches_back, BLOCKS - 1 - late_block + part, part - 1),
        )
        return q_half, q_block, k_half, k_block

    def for_blocks(step, work):
        @pl.when(step < EARLY_STEPS)
        def _():
            work(0, step)
            work(0, BLOCKS - 1 - step)

        @pl.when(step >= EARLY_STEPS)
        def _():
            work(1, step - EARLY_STEPS)

    def each_owner(block, work):
        for part in range(PER_BLOCK):
            shard = block * PER_BLOCK + part

            @pl.when(shard != me)
            def _():
                work(shard, False)

            @pl.when(shard == me)
            def _():
                work(shard, True)

    def deliver(src, dst, kind, half, shard, here):
        if here:
            dst[...] = src[...]
        else:
            push(src, dst, kind, half, shard)

    @pl.when(works)
    def _():
        ends = []
        total = 0
        for user in range(lengths.shape[1]):
            total = total + lengths[0, user]
            ends.append(total)

        def bounds_step(index, carry):
            half, block = index // BLOCKS, index % BLOCKS
            q_time = times(half, block, (BLOCK, HEAD), 0)
            first = jnp.zeros((BLOCK, HEAD), jnp.int32)
            for end in ends:
                first = jnp.where(q_time >= end, end, first)
            bounds[0, half, block] = first
            bounds[1, half, block] = q_time
            return carry

        lax.fori_loop(0, 2 * BLOCKS, bounds_step, 0)
        sums[...] = jnp.zeros(sums.shape, jnp.float32)
        dq_sum[...] = jnp.zeros(dq_sum.shape, jnp.float32)
        att_sum[...] = jnp.zeros(att_sum.shape, jnp.float32)
        landed(box.at[:2, :, others], QUERY_KEY)

        def score_step(step, carry):
            for part in range(PARTS):
                q_half, q_block, k_half, k_block = pair(step, part)
                k_time = times(k_half, k_block, (1, BLOCK), 1)
                first = jnp.tile(bounds[0, q_half, q_block], (1, BLOCK // HEAD))
                q_time = jnp.tile(bounds[1, q_half, q_block], (1, BLOCK // HEAD))
                raw = contract(rows_of(0, q_half, q_block), rows_of(1, k_half, k_block), 1, 1)
                scores = raw * SCALE
                live = (k_time >= first) & (k_time <= q_time)
                sigmoid = 0.5 * jnp.tanh(raw * (0.5 * SCALE)) + 0.5
                silu = scores * sigmoid
                slope = sigmoid * SCALE + silu * (SCALE - SCALE * sigmoid)
                weights[step, part] = jnp.where(live, silu, 0.0).astype(jnp.bfloat16)
                slopes[step, part] = jnp.where(live, slope, 0.0)
            return carry

        lax.fori_loop(0, STEPS, score_step, 0)

    @pl.when(works)
    def _():
        landed(box.at[2, :, others], VALUE)

        def attend_step(step, carry):
            for part in range(PARTS):
                q_half, q_block, k_half, k_block = pair(step, part)
                att_sum[place_of(q_half, q_block), :] += contract(
                    weights[step, part], rows_of(2, k_half, k_block), 1, 0
                )

            def send(half, block):
                att_out[half, chunks(block)] = (
                    att_sum[place_of(half, block), :]
                    .astype(jnp.bfloat16)
                    .reshape(PER_BLOCK, CHUNK, HEAD)
                )
                each_owner(
                    block,
                    lambda shard, here: deliver(
                        att_out.at[half, shard],
                        att_in.at[half, :, columns(head)],
                        ATT,
                        half,
                        shard,
                        here,
                    ),
                )

            for_blocks(step, send)
            return carry

        lax.fori_loop(0, STEPS, attend_step, 0)

    def flip(matrix):
        return matrix.astype(jnp.float32).T.astype(jnp.bfloat16)

    @pl.when(works)
    def _():
        def flip_step(block, carry):
            for half in range(2):
                q_flipped[half, block] = flip(rows_of(0, half, block))
            return carry

        lax.fori_loop(0, BLOCKS, flip_step, 0)

    for copy in staged[4:]:
        copy.wait()
    gain_row = gain[...]

    def normalize_half(half):
        by_count(lambda count: landed(att_in.at[half, :, : count * HEAD], ATT, half))

        def normalize(part, gain_sum):
            rows = pl.ds(pl.multiple_of(part * 32, 32), 32)
            attended = att_in[half, rows, :].astype(jnp.float32)
            centered = attended - jnp.mean(attended, axis=1, keepdims=True)
            variance = jnp.mean(centered * centered, axis=1, keepdims=True)
            inverse = lax.rsqrt(variance + EPSILON)
            normed = centered * inverse
            gate = gates[half, rows, :].astype(jnp.float32)
            grad = cotangent[half, rows, :].astype(jnp.float32)
            scaled = gate * gain_row
            output[half, rows, :] = (normed * scaled).astype(jnp.bfloat16)
            gain_sum = gain_sum + jnp.sum(normed * grad * gate, axis=0, keepdims=True)
            grad = grad * scaled
            grad_out[half, rows, :] = (
                (
                    grad
                    - jnp.mean(grad, axis=1, keepdims=True)
                    - normed * jnp.mean(grad * normed, axis=1, keepdims=True)
                )
                * inverse
            ).astype(jnp.bfloat16)
            return gain_sum

        gain_sum = lax.fori_loop(
            0, CHUNK // 32, normalize, jnp.zeros((1, gain.shape[1]), jnp.float32)
        )
        each_worker(
            lambda which, peer: push(
                grad_out.at[half, :, columns(which)], grad_in.at[half, me], GRAD, half, peer
            )
        )

        @pl.when(works)
        def _():
            grad_in[half, me] = grad_out[half, :, columns(head)]

        return gain_sum

    gain_sum = normalize_half(0)
    gain_sum = gain_sum + normalize_half(1)
    output_copy = pltpu.make_async_copy(output, output_hbm, out_sem.at[0])
    output_copy.start()

    both, along = PEERS, PEERS + 2

    def gain_copy(slots, kind, target):
        return pltpu.make_async_remote_copy(
            src_ref=slots,
            dst_ref=slots,
            send_sem=send_sem.at[kind, 0],
            recv_sem=recv_sem.at[kind, 0],
            device_id=target,
            device_id_type=MESH,
        )

    for which in range(HEADS):
        gain_slots[me, which : which + 1, :] = gain_sum[:, which * HEAD : (which + 1) * HEAD]

    def send_gain(turn, carry):
        adder = 2 * lax.rem(head + turn, HEADS) + 1 - core
        push(gain_slots.at[me], gain_slots.at[me], GAIN, 0, adder)
        return carry

    lax.fori_loop(jnp.where(works, 0, 1), HEADS, send_gain, 0)

    def gain_over_groups():
        landed(gain_slots.at[others], GAIN)
        gain_slots[both + core] = jnp.sum(gain_slots[:PEERS], axis=0)
        gain_copy(gain_slots.at[both + core], GAIN_CORE, near[0]).start()
        gain_copy(gain_slots.at[both], GAIN_CORE, near[0]).wait_recv()
        mine = along + place_z
        gain_slots[mine] = gain_slots[both] + gain_slots[both + 1]

        def send(distance, carry):
            gain_copy(gain_slots.at[mine], GAIN_LAYER, {"dp": layer(distance)}).start()
            return carry

        if layers > 1:
            lax.fori_loop(1, layers, send, 0)
            gain_copy(gain_slots.at[along : along + layers - 1], GAIN_LAYER, near[0]).wait_recv()
        gain_total[...] = jnp.sum(gain_slots[along : along + layers], axis=0)
        push(gain_total, gain_total, GAIN_TOTAL, 0, mate)

    def finish(half, block):
        for index in range(2):
            out_box[1 + index, half, chunks(block)] = (
                sums[index, :, place_of(half, block)]
                .T.astype(jnp.bfloat16)
                .reshape(PER_BLOCK, CHUNK, HEAD)
            )

    def backward_step(step, carry):
        def prepare(half, block):
            grad_flipped[half, block] = flip(grad_in[half, chunks(block)].reshape(BLOCK, HEAD))

        for_blocks(step, prepare)
        for part in range(PARTS):
            q_half, q_block, k_half, k_block = pair(step, part)
            grad = grad_in[q_half, chunks(q_block)].reshape(BLOCK, HEAD)
            place = place_of(k_half, k_block)
            grad_weights = contract(grad, rows_of(2, k_half, k_block), 1, 1)
            grad_scores = (grad_weights * slopes[step, part]).astype(jnp.bfloat16)
            sums[0, :, place] += contract(q_flipped[q_half, q_block], grad_scores, 1, 0)
            sums[1, :, place] += contract(grad_flipped[q_half, q_block], weights[step, part], 1, 0)
            dq_sum[place_of(q_half, q_block), :] += contract(
                grad_scores, rows_of(1, k_half, k_block), 1, 0
            )

        def send_queries(half, block):
            out_box[0, half, chunks(block)] = (
                dq_sum[place_of(half, block), :]
                .astype(jnp.bfloat16)
                .reshape(PER_BLOCK, CHUNK, HEAD)
            )
            if half == 1:
                finish(1, block)
            count = 1 + 2 * half
            each_owner(
                block,
                lambda shard, here: deliver(
                    out_box.at[:count, half, shard],
                    back.at[:count, half, :, columns(head)],
                    DQ,
                    half,
                    shard,
                    here,
                ),
            )

        for_blocks(step, send_queries)
        return carry

    pl.when(jnp.logical_not(works))(gain_over_groups)

    @pl.when(works)
    def _():
        landed(grad_in.at[0, others], GRAD, 0)

        def wait_and_step(step, carry):
            @pl.when(step == EARLY_STEPS)
            def _():
                landed(grad_in.at[1, others], GRAD, 1)

            return backward_step(step, carry)

        lax.fori_loop(0, STEPS, wait_and_step, 0)

        def finish_early(block, carry):
            finish(0, block)
            each_owner(
                block,
                lambda shard, here: deliver(
                    out_box.at[1:, 0, shard],
                    back.at[1:, 0, :, columns(head)],
                    DKV,
                    0,
                    shard,
                    here,
                ),
            )
            return carry

        lax.fori_loop(0, BLOCKS, finish_early, 0)

    def wait_back(count):
        cols = slice(0, count * HEAD)
        landed(back.at[0, 0, :, cols], DQ, 0)
        landed(back.at[:, 1, :, cols], DQ, 1)
        landed(back.at[1:, 0, :, cols], DKV)

    by_count(wait_back)
    results = [
        pltpu.make_async_copy(back.at[index], result, out_sem.at[1 + index])
        for index, result in enumerate((grad_queries_hbm, grad_keys_hbm, grad_values_hbm))
    ]
    for copy in results:
        copy.start()
    pl.when(works)(lambda: landed(gain_total, GAIN_TOTAL))
    results.append(pltpu.make_async_copy(gain_total, gain_total_hbm, out_sem.at[4]))
    results[-1].start()

    @pl.when(works)
    def _():
        for half in range(2):
            left(att_out.at[half, others], ATT, half)
        left(out_box.at[0, 0, others], DQ, 0)
        left(out_box.at[:, 1, others], DQ, 1)
        left(out_box.at[1:, 0, others], DKV)

    def inputs_left(count):
        left(box.at[2, :, :count], VALUE)
        for half in range(2):
            left(grad_in.at[half, :count], GRAD, half)

    by_count(inputs_left)

    @pl.when(works)
    def _():
        left(gain_slots.at[:HEADS], GAIN)

    @pl.when(jnp.logical_not(works))
    def _():
        left(gain_slots.at[: HEADS - 1], GAIN)
        gain_copy(gain_slots.at[both], GAIN_CORE, near[0]).wait_send()
        if layers > 1:
            gain_copy(gain_slots.at[along : along + layers - 1], GAIN_LAYER, near[0]).wait_send()
        left(gain_total, GAIN_TOTAL)

    output_copy.wait()
    for copy in results:
        copy.wait()


def hand_over(*refs):
    count = (len(refs) - 1) // 2
    copies = [
        pltpu.make_async_copy(src, dst, refs[-1].at[index])
        for index, (src, dst) in enumerate(zip(refs[:count], refs[count : 2 * count]))
    ]
    for copy in copies:
        copy.start()
    for copy in copies:
        copy.wait()


def body(queries, key_vectors, value_vectors, gate_values, cotangent, norm_gain, lengths):
    row_count, width = queries.shape
    groups = lax.axis_size("dp")
    halves = (2, CHUNK, width)
    wide = jax.ShapeDtypeStruct(halves, jnp.bfloat16)
    vmem = pl.BlockSpec(memory_space=pltpu.VMEM)
    hbm = pl.BlockSpec(memory_space=pltpu.HBM)
    boxes = (2, PEERS, CHUNK, HEAD)

    def kernel(*refs):
        attention_kernel(groups, *refs)

    shapes = (wide, wide, wide, wide, jax.ShapeDtypeStruct((HEADS, HEAD), jnp.float32))
    results = pl.pallas_call(
        kernel,
        out_shape=shapes,
        in_specs=[hbm] * 7,
        out_specs=(hbm,) * 5,
        scratch_shapes=[
            pltpu.SMEM(lengths.shape, jnp.int32),
            pltpu.VMEM((3,) + halves, jnp.bfloat16),
            pltpu.VMEM(halves, jnp.bfloat16),
            pltpu.VMEM(halves, jnp.bfloat16),
            pltpu.VMEM((1, width), jnp.float32),
            pltpu.VMEM((3,) + boxes, jnp.bfloat16),
            pltpu.VMEM((2, 2, BLOCKS, BLOCK, HEAD), jnp.int32),
            pltpu.VMEM((STEPS, PARTS, BLOCK, BLOCK), jnp.bfloat16),
            pltpu.VMEM((STEPS, PARTS, BLOCK, BLOCK), jnp.float32),
            pltpu.VMEM((2 * HALF, HEAD), jnp.float32),
            pltpu.VMEM(boxes, jnp.bfloat16),
            pltpu.VMEM(halves, jnp.bfloat16),
            pltpu.VMEM(halves, jnp.bfloat16),
            pltpu.VMEM(halves, jnp.bfloat16),
            pltpu.VMEM(boxes, jnp.bfloat16),
            pltpu.VMEM((2, BLOCKS, HEAD, BLOCK), jnp.bfloat16),
            pltpu.VMEM((2, BLOCKS, HEAD, BLOCK), jnp.bfloat16),
            pltpu.VMEM((2 * HALF, HEAD), jnp.float32),
            pltpu.VMEM((2, HEAD, 2 * HALF), jnp.float32),
            pltpu.VMEM((3,) + boxes, jnp.bfloat16),
            pltpu.VMEM((3,) + halves, jnp.bfloat16),
            pltpu.VMEM((PEERS + 2 + groups // 2, HEADS, HEAD), jnp.float32),
            pltpu.VMEM((HEADS, HEAD), jnp.float32),
            pltpu.SemaphoreType.DMA((7,)),
            pltpu.SemaphoreType.DMA((5,)),
            pltpu.SemaphoreType.DMA((KINDS, 2)),
            pltpu.SemaphoreType.DMA((KINDS, 2)),
            pltpu.SemaphoreType.REGULAR((8,)),
        ],
        compiler_params=pltpu.CompilerParams(
            collective_id=0, has_side_effects=True, vmem_limit_bytes=60 * 2**20
        ),
    )(
        lengths,
        *(
            array.reshape(halves)
            for array in (queries, key_vectors, value_vectors, gate_values, cotangent)
        ),
        norm_gain.reshape(1, width),
    )
    *grads, gain_total = pl.pallas_call(
        hand_over,
        out_shape=shapes,
        in_specs=[vmem] * 5,
        out_specs=(hbm,) * 5,
        scratch_shapes=[pltpu.SemaphoreType.DMA((5,))],
    )(*results)
    return *(array.reshape(row_count, width) for array in grads), gain_total.reshape(width)


def solution(mesh):
    rows = P(("dp", "ctx"), None)
    return jax.shard_map(
        body,
        mesh=mesh,
        in_specs=(rows,) * 5 + (P(), P("dp", None)),
        out_specs=(rows,) * 4 + (P(),),
        check_vma=False,
    )
```

```python
import math

import jax
import jax.numpy as jnp
from jax import lax
from jax.experimental import pallas as pl
from jax.experimental.pallas import tpu as pltpu
from jax.sharding import PartitionSpec as P

HEAD = 128
EPSILON = 1e-05
PEERS = 16
HEADS = 8
CHUNK = 64
HALF = PEERS * CHUNK
BLOCK = 256
PER_BLOCK = BLOCK // CHUNK
BLOCKS = HALF // BLOCK
PARTS = BLOCKS + 1
ROW = 4
ROWS_OF_PEERS = PEERS // ROW
EARLY_STEPS = BLOCKS // 2
STEPS = EARLY_STEPS + BLOCKS
SCALE = 1.0 / math.sqrt(HEAD)

QUERY_KEY, VALUE, ATT, GRAD, DQ, DKV, GAIN, GAIN_LAYER, GAIN_TOTAL = range(9)
KINDS = 9
MESH = pl.DeviceIdType.MESH


def contract(left, right, left_axis, right_axis):
    return lax.dot_general(
        left, right, (((left_axis,), (right_axis,)), ((), ())), preferred_element_type=jnp.float32
    )


def attention_kernel(
    groups,
    lengths_hbm,
    queries_hbm,
    keys_hbm,
    values_hbm,
    gates_hbm,
    cotangent_hbm,
    gain_hbm,
    output_hbm,
    grad_queries_hbm,
    grad_keys_hbm,
    grad_values_hbm,
    gain_total_hbm,
    lengths,
    own,
    gates,
    cotangent,
    gain,
    box,
    bounds,
    weights,
    slopes,
    att_sum,
    att_out,
    att_in,
    output,
    grad_out,
    grad_in,
    q_flipped,
    grad_flipped,
    dq_sum,
    sums,
    out_box,
    back,
    gain_slots,
    gain_total,
    local_sem,
    out_sem,
    send_sem,
    recv_sem,
    grad_sem,
    word_sem,
):
    me = lax.axis_index("ctx")
    group = lax.axis_index("dp")
    core = group % 2
    head = me // 2
    works = me % 2 == core
    place_z, layers = group // 2, groups // 2
    row, adder_place = me // ROW, 1 + core
    adds = me % ROW == adder_place
    partner = group + 1 - 2 * core
    others = slice(0, PEERS - 1)

    staged = [
        pltpu.make_async_copy(src, dst, local_sem.at[index])
        for index, (src, dst) in enumerate(
            (
                (queries_hbm, own.at[0]),
                (keys_hbm, own.at[1]),
                (values_hbm, own.at[2]),
                (lengths_hbm, lengths),
                (gates_hbm, gates),
                (cotangent_hbm, cotangent),
                (gain_hbm, gain),
            )
        )
    ]
    for copy in staged:
        copy.start()

    def columns(which):
        return pl.ds(pl.multiple_of(which * HEAD, HEAD), HEAD)

    def remote(src, dst, kind, half, target):
        return pltpu.make_async_remote_copy(
            src_ref=src,
            dst_ref=dst,
            send_sem=send_sem.at[kind, half],
            recv_sem=recv_sem.at[kind, half],
            device_id={"ctx": target},
            device_id_type=MESH,
        )

    def push(src, dst, kind, half, target):
        remote(src, dst, kind, half, target).start()

    def landed(ref, kind, half=0):
        remote(ref, ref, kind, half, me).wait_recv()

    def left(ref, kind, half=0):
        remote(ref, ref, kind, half, me).wait_send()

    def layer(distance):
        return 2 * lax.rem(place_z + distance + layers, layers) + core

    barrier = pltpu.get_barrier_semaphore()
    for turn in range(1, PEERS):
        pl.semaphore_signal(
            barrier, inc=1, device_id={"ctx": lax.rem(me + turn, PEERS)}, device_id_type=MESH
        )
    near = [{"dp": partner, "ctx": row * ROW + 2 - core}]
    if layers > 1:
        near += [{"dp": layer(1)}, {"dp": layer(-1)}]

    @pl.when(adds)
    def _():
        for peer in near:
            pl.semaphore_signal(barrier, inc=1, device_id=peer, device_id_type=MESH)

    for copy in staged[:4]:
        copy.wait()

    @pl.when(jnp.logical_not(adds))
    def _():
        pl.semaphore_wait(barrier, PEERS - 1)

    @pl.when(adds)
    def _():
        pl.semaphore_wait(barrier, PEERS - 1 + len(near))

    rounds = [1 << index for index in range(8) if 1 << index < layers // 2 + layers % 2]

    def row_mates(work):
        for turn in range(1, ROW):
            work(row * ROW + (me + turn) % ROW)

    def pass_words():
        pl.semaphore_signal(word_sem.at[6], inc=1, device_id=near[0], device_id_type=MESH)
        pl.semaphore_wait(word_sem.at[6], 1)
        row_mates(
            lambda peer: pl.semaphore_signal(
                word_sem.at[7], inc=1, device_id={"ctx": peer}, device_id_type=MESH
            )
        )
        for index, reach in enumerate(rounds):
            for distance in (reach, -reach):
                pl.semaphore_signal(
                    word_sem.at[index], inc=1, device_id={"dp": layer(distance)}, device_id_type=MESH
                )
            pl.semaphore_wait(word_sem.at[index], 2)

    def each_worker(work):
        def step(turn, carry):
            which = lax.rem(head + turn, HEADS)
            work(which, 2 * which + core)
            return carry

        lax.fori_loop(jnp.where(works, 1, 0), HEADS, step, 0)

    def by_count(work):
        @pl.when(works)
        def _():
            work(HEADS - 1)

        @pl.when(jnp.logical_not(works))
        def _():
            work(HEADS)

    for half in range(2):
        each_worker(
            lambda which, peer: push(
                own.at[:2, half, :, columns(which)], box.at[:2, half, me], QUERY_KEY, half, peer
            )
        )

    @pl.when(works)
    def _():
        box[:, :, me] = own[:, :, :, columns(head)]

    def queries_keys_left(count):
        for half in range(2):
            left(box.at[:2, half, :count], QUERY_KEY, half)

    by_count(queries_keys_left)
    each_worker(
        lambda which, peer: push(own.at[2, :, :, columns(which)], box.at[2, :, me], VALUE, 0, peer)
    )
    pl.when(adds)(pass_words)

    def times(half, block, shape, axis):
        place = lax.broadcasted_iota(jnp.int32, shape, axis)
        chunk, inner = place // CHUNK, place % CHUNK
        shard = block * PER_BLOCK + chunk
        return jnp.where(half == 0, shard, 2 * PEERS - 1 - shard) * CHUNK + inner

    def rows_of(which, half, block):
        start = pl.multiple_of(block * PER_BLOCK, PER_BLOCK)
        return box[which, half, pl.ds(start, PER_BLOCK)].reshape(BLOCK, HEAD)

    def chunks(block):
        return pl.ds(pl.multiple_of(block * PER_BLOCK, PER_BLOCK), PER_BLOCK)

    def place_of(half, block):
        return pl.ds(pl.multiple_of(half * HALF + block * BLOCK, BLOCK), BLOCK)

    def pair(step, part):
        early = step < EARLY_STEPS
        short = part <= step
        late_block = step - EARLY_STEPS
        reaches_back = part <= late_block
        q_half = jnp.where(early, 0, 1)
        q_block = jnp.where(early, jnp.where(short, step, BLOCKS - 1 - step), late_block)
        k_half = jnp.where(early | reaches_back, 0, 1)
        k_block = jnp.where(
            early,
            jnp.where(short, part, part - step - 1),
            jnp.where(reaches_back, BLOCKS - 1 - late_block + part, part - 1),
        )
        return q_half, q_block, k_half, k_block

    def for_blocks(step, work):
        @pl.when(step < EARLY_STEPS)
        def _():
            work(0, step)
            work(0, BLOCKS - 1 - step)

        @pl.when(step >= EARLY_STEPS)
        def _():
            work(1, step - EARLY_STEPS)

    def each_owner(block, work):
        for part in range(PER_BLOCK):
            shard = block * PER_BLOCK + part

            @pl.when(shard != me)
            def _():
                work(shard, False)

            @pl.when(shard == me)
            def _():
                work(shard, True)

    def deliver(src, dst, kind, half, shard, here):
        if here:
            dst[...] = src[...]
        else:
            push(src, dst, kind, half, shard)

    @pl.when(works)
    def _():
        ends = []
        total = 0
        for user in range(lengths.shape[1]):
            total = total + lengths[0, user]
            ends.append(total)

        def bounds_step(index, carry):
            half, block = index // BLOCKS, index % BLOCKS
            q_time = times(half, block, (BLOCK, HEAD), 0)
            first = jnp.zeros((BLOCK, HEAD), jnp.int32)
            for end in ends:
                first = jnp.where(q_time >= end, end, first)
            bounds[0, half, block] = first
            bounds[1, half, block] = q_time
            return carry

        lax.fori_loop(0, 2 * BLOCKS, bounds_step, 0)
        sums[...] = jnp.zeros(sums.shape, jnp.float32)
        dq_sum[...] = jnp.zeros(dq_sum.shape, jnp.float32)
        att_sum[...] = jnp.zeros(att_sum.shape, jnp.float32)
        landed(box.at[:2, 0, others], QUERY_KEY, 0)

        def score_step(step, carry):
            for part in range(PARTS):
                q_half, q_block, k_half, k_block = pair(step, part)
                k_time = times(k_half, k_block, (1, BLOCK), 1)
                first = jnp.tile(bounds[0, q_half, q_block], (1, BLOCK // HEAD))
                q_time = jnp.tile(bounds[1, q_half, q_block], (1, BLOCK // HEAD))
                raw = contract(rows_of(0, q_half, q_block), rows_of(1, k_half, k_block), 1, 1)
                scores = raw * SCALE
                live = (k_time >= first) & (k_time <= q_time)
                sigmoid = 0.5 * jnp.tanh(raw * (0.5 * SCALE)) + 0.5
                silu = scores * sigmoid
                slope = sigmoid * SCALE + silu * (SCALE - SCALE * sigmoid)
                weights[step, part] = jnp.where(live, silu, 0.0).astype(jnp.bfloat16)
                slopes[step, part] = jnp.where(live, slope, 0.0)
            return carry

        lax.fori_loop(0, EARLY_STEPS, score_step, 0)
        landed(box.at[:2, 1, others], QUERY_KEY, 1)
        lax.fori_loop(EARLY_STEPS, STEPS, score_step, 0)

    @pl.when(works)
    def _():
        landed(box.at[2, :, others], VALUE)

        def attend_step(step, carry):
            for part in range(PARTS):
                q_half, q_block, k_half, k_block = pair(step, part)
                att_sum[place_of(q_half, q_block), :] += contract(
                    weights[step, part], rows_of(2, k_half, k_block), 1, 0
                )

            def send(half, block):
                att_out[half, chunks(block)] = (
                    att_sum[place_of(half, block), :]
                    .astype(jnp.bfloat16)
                    .reshape(PER_BLOCK, CHUNK, HEAD)
                )
                each_owner(
                    block,
                    lambda shard, here: deliver(
                        att_out.at[half, shard],
                        att_in.at[half, :, columns(head)],
                        ATT,
                        half,
                        shard,
                        here,
                    ),
                )

            for_blocks(step, send)
            return carry

        lax.fori_loop(0, STEPS, attend_step, 0)

    def flip(matrix):
        return matrix.astype(jnp.float32).T.astype(jnp.bfloat16)

    @pl.when(works)
    def _():
        def flip_step(block, carry):
            for half in range(2):
                q_flipped[half, block] = flip(rows_of(0, half, block))
            return carry

        lax.fori_loop(0, BLOCKS, flip_step, 0)

    for copy in staged[4:]:
        copy.wait()
    gain_row = gain[...]

    def grad_copy(src, dst, half, block, target):
        return pltpu.make_async_remote_copy(
            src_ref=src,
            dst_ref=dst,
            send_sem=send_sem.at[GRAD, half],
            recv_sem=grad_sem.at[half, block],
            device_id={"ctx": target},
            device_id_type=MESH,
        )

    def grads_landed(half, block):
        @pl.when(me // PER_BLOCK == block)
        def _():
            rest = grad_in.at[half, : PER_BLOCK - 1]
            grad_copy(rest, rest, half, block, me).wait_recv()

        @pl.when(me // PER_BLOCK != block)
        def _():
            rest = grad_in.at[half, :PER_BLOCK]
            grad_copy(rest, rest, half, block, me).wait_recv()

    along = 2 * PEERS

    def gain_copy(slots, kind, target):
        return pltpu.make_async_remote_copy(
            src_ref=slots,
            dst_ref=slots,
            send_sem=send_sem.at[kind, 0],
            recv_sem=recv_sem.at[kind, 0],
            device_id=target,
            device_id_type=MESH,
        )

    def send_gain(gain_sum):
        mine = core * PEERS + me
        for which in range(HEADS):
            gain_slots[mine, which : which + 1, :] = gain_sum[:, which * HEAD : (which + 1) * HEAD]
        pl.when(jnp.logical_not(adds))(lambda: pl.semaphore_wait(word_sem.at[7], 1))
        for turn in range(ROWS_OF_PEERS):
            start = (row + turn) % ROWS_OF_PEERS * ROW
            if turn == 0:

                @pl.when(jnp.logical_not(adds))
                def _():
                    gain_copy(gain_slots.at[mine], GAIN, {"ctx": start + adder_place}).start()

            else:
                gain_copy(gain_slots.at[mine], GAIN, {"ctx": start + adder_place}).start()
            other = {"dp": partner, "ctx": start + 2 - core}
            gain_copy(gain_slots.at[mine], GAIN, other).start()

    def gain_over_groups():
        gain_copy(gain_slots.at[: 2 * PEERS - 1], GAIN, near[0]).wait_recv()
        mine = along + place_z
        gain_slots[mine] = jnp.sum(gain_slots[: 2 * PEERS], axis=0)

        def send(distance, carry):
            gain_copy(gain_slots.at[mine], GAIN_LAYER, {"dp": layer(distance)}).start()
            return carry

        if layers > 1:
            lax.fori_loop(1, layers, send, 0)
            gain_copy(gain_slots.at[along : along + layers - 1], GAIN_LAYER, near[0]).wait_recv()
        gain_total[...] = jnp.sum(gain_slots[along : along + layers], axis=0)
        row_mates(lambda peer: push(gain_total, gain_total, GAIN_TOTAL, 0, peer))

    def normalize_half(half, gain_before):
        by_count(lambda count: landed(att_in.at[half, :, : count * HEAD], ATT, half))

        def normalize(part, gain_sum):
            rows = pl.ds(pl.multiple_of(part * 32, 32), 32)
            attended = att_in[half, rows, :].astype(jnp.float32)
            centered = attended - jnp.mean(attended, axis=1, keepdims=True)
            variance = jnp.mean(centered * centered, axis=1, keepdims=True)
            inverse = lax.rsqrt(variance + EPSILON)
            normed = centered * inverse
            gate = gates[half, rows, :].astype(jnp.float32)
            grad = cotangent[half, rows, :].astype(jnp.float32)
            scaled = gate * gain_row
            output[half, rows, :] = (normed * scaled).astype(jnp.bfloat16)
            gain_sum = gain_sum + jnp.sum(normed * grad * gate, axis=0, keepdims=True)
            grad = grad * scaled
            grad_out[half, rows, :] = (
                (
                    grad
                    - jnp.mean(grad, axis=1, keepdims=True)
                    - normed * jnp.mean(grad * normed, axis=1, keepdims=True)
                )
                * inverse
            ).astype(jnp.bfloat16)
            return gain_sum

        gain_sum = lax.fori_loop(
            0, CHUNK // 32, normalize, gain_before
        )
        if half == 1:
            send_gain(gain_sum)
        each_worker(
            lambda which, peer: grad_copy(
                grad_out.at[half, :, columns(which)], grad_in.at[half, me], half, me // PER_BLOCK, peer
            ).start()
        )

        @pl.when(works)
        def _():
            grad_in[half, me] = grad_out[half, :, columns(head)]

        return gain_sum

    normalize_half(1, normalize_half(0, jnp.zeros((1, gain.shape[1]), jnp.float32)))
    output_copy = pltpu.make_async_copy(output, output_hbm, out_sem.at[0])
    output_copy.start()

    def finish(half, block):
        for index in range(2):
            out_box[1 + index, half, chunks(block)] = (
                sums[index, :, place_of(half, block)]
                .T.astype(jnp.bfloat16)
                .reshape(PER_BLOCK, CHUNK, HEAD)
            )

    def backward_step(step, carry):
        def prepare(half, block):
            grads_landed(half, block)
            grad_flipped[half, block] = flip(grad_in[half, chunks(block)].reshape(BLOCK, HEAD))

        for_blocks(step, prepare)
        for part in range(PARTS):
            q_half, q_block, k_half, k_block = pair(step, part)
            grad = grad_in[q_half, chunks(q_block)].reshape(BLOCK, HEAD)
            place = place_of(k_half, k_block)
            grad_weights = contract(grad, rows_of(2, k_half, k_block), 1, 1)
            grad_scores = (grad_weights * slopes[step, part]).astype(jnp.bfloat16)
            sums[0, :, place] += contract(q_flipped[q_half, q_block], grad_scores, 1, 0)
            sums[1, :, place] += contract(grad_flipped[q_half, q_block], weights[step, part], 1, 0)
            dq_sum[place_of(q_half, q_block), :] += contract(
                grad_scores, rows_of(1, k_half, k_block), 1, 0
            )

        def send_queries(half, block):
            out_box[0, half, chunks(block)] = (
                dq_sum[place_of(half, block), :]
                .astype(jnp.bfloat16)
                .reshape(PER_BLOCK, CHUNK, HEAD)
            )
            if half == 1:
                finish(1, block)
            count = 1 + 2 * half
            each_owner(
                block,
                lambda shard, here: deliver(
                    out_box.at[:count, half, shard],
                    back.at[:count, half, :, columns(head)],
                    DQ,
                    half,
                    shard,
                    here,
                ),
            )

        for_blocks(step, send_queries)
        return carry

    pl.when(adds)(gain_over_groups)

    @pl.when(works)
    def _():
        lax.fori_loop(0, STEPS, backward_step, 0)

        def finish_early(block, carry):
            finish(0, block)
            each_owner(
                block,
                lambda shard, here: deliver(
                    out_box.at[1:, 0, shard],
                    back.at[1:, 0, :, columns(head)],
                    DKV,
                    0,
                    shard,
                    here,
                ),
            )
            return carry

        lax.fori_loop(0, BLOCKS, finish_early, 0)

    def wait_back(count):
        cols = slice(0, count * HEAD)
        landed(back.at[0, 0, :, cols], DQ, 0)
        landed(back.at[:, 1, :, cols], DQ, 1)
        landed(back.at[1:, 0, :, cols], DKV)

    by_count(wait_back)
    results = [
        pltpu.make_async_copy(back.at[index], result, out_sem.at[1 + index])
        for index, result in enumerate((grad_queries_hbm, grad_keys_hbm, grad_values_hbm))
    ]
    for copy in results:
        copy.start()
    pl.when(jnp.logical_not(adds))(lambda: landed(gain_total, GAIN_TOTAL))
    results.append(pltpu.make_async_copy(gain_total, gain_total_hbm, out_sem.at[4]))
    results[-1].start()

    @pl.when(works)
    def _():
        for half in range(2):
            left(att_out.at[half, others], ATT, half)
        left(out_box.at[0, 0, others], DQ, 0)
        left(out_box.at[:, 1, others], DQ, 1)
        left(out_box.at[1:, 0, others], DKV)

    def inputs_left(count):
        left(box.at[2, :, :count], VALUE)
        for half in range(2):
            left(grad_in.at[half, :count], GRAD, half)

    by_count(inputs_left)

    @pl.when(jnp.logical_not(adds))
    def _():
        left(gain_slots.at[: 2 * ROWS_OF_PEERS], GAIN)

    @pl.when(adds)
    def _():
        left(gain_slots.at[: 2 * ROWS_OF_PEERS - 1], GAIN)
        if layers > 1:
            gain_copy(gain_slots.at[along : along + layers - 1], GAIN_LAYER, near[0]).wait_send()
        left(gain_slots.at[: ROW - 1], GAIN_TOTAL)

    output_copy.wait()
    for copy in results:
        copy.wait()


def hand_over(*refs):
    count = (len(refs) - 2) // 3
    sources, results, held = refs[:count], refs[count : 2 * count], refs[2 * count : 3 * count]
    into = [
        pltpu.make_async_copy(src, dst, refs[-2].at[index])
        for index, (src, dst) in enumerate(zip(sources, held))
    ]
    out = [
        pltpu.make_async_copy(src, dst, refs[-1].at[index])
        for index, (src, dst) in enumerate(zip(held, results))
    ]
    for copy in into:
        copy.start()
    for copy, after in zip(into, out):
        copy.wait()
        after.start()
    for copy in out:
        copy.wait()


def body(queries, key_vectors, value_vectors, gate_values, cotangent, norm_gain, lengths):
    row_count, width = queries.shape
    groups = lax.axis_size("dp")
    halves = (2, CHUNK, width)
    wide = jax.ShapeDtypeStruct(halves, jnp.bfloat16)
    hbm = pl.BlockSpec(memory_space=pltpu.HBM)
    boxes = (2, PEERS, CHUNK, HEAD)

    def kernel(*refs):
        attention_kernel(groups, *refs)

    shapes = (wide, wide, wide, wide, jax.ShapeDtypeStruct((HEADS, HEAD), jnp.float32))
    results = pl.pallas_call(
        kernel,
        out_shape=shapes,
        in_specs=[hbm] * 7,
        out_specs=(hbm,) * 5,
        scratch_shapes=[
            pltpu.SMEM(lengths.shape, jnp.int32),
            pltpu.VMEM((3,) + halves, jnp.bfloat16),
            pltpu.VMEM(halves, jnp.bfloat16),
            pltpu.VMEM(halves, jnp.bfloat16),
            pltpu.VMEM((1, width), jnp.float32),
            pltpu.VMEM((3,) + boxes, jnp.bfloat16),
            pltpu.VMEM((2, 2, BLOCKS, BLOCK, HEAD), jnp.int32),
            pltpu.VMEM((STEPS, PARTS, BLOCK, BLOCK), jnp.bfloat16),
            pltpu.VMEM((STEPS, PARTS, BLOCK, BLOCK), jnp.float32),
            pltpu.VMEM((2 * HALF, HEAD), jnp.float32),
            pltpu.VMEM(boxes, jnp.bfloat16),
            pltpu.VMEM(halves, jnp.bfloat16),
            pltpu.VMEM(halves, jnp.bfloat16),
            pltpu.VMEM(halves, jnp.bfloat16),
            pltpu.VMEM(boxes, jnp.bfloat16),
            pltpu.VMEM((2, BLOCKS, HEAD, BLOCK), jnp.bfloat16),
            pltpu.VMEM((2, BLOCKS, HEAD, BLOCK), jnp.bfloat16),
            pltpu.VMEM((2 * HALF, HEAD), jnp.float32),
            pltpu.VMEM((2, HEAD, 2 * HALF), jnp.float32),
            pltpu.VMEM((3,) + boxes, jnp.bfloat16),
            pltpu.VMEM((3,) + halves, jnp.bfloat16),
            pltpu.VMEM((2 * PEERS + groups // 2, HEADS, HEAD), jnp.float32),
            pltpu.VMEM((HEADS, HEAD), jnp.float32),
            pltpu.SemaphoreType.DMA((7,)),
            pltpu.SemaphoreType.DMA((5,)),
            pltpu.SemaphoreType.DMA((KINDS, 2)),
            pltpu.SemaphoreType.DMA((KINDS, 2)),
            pltpu.SemaphoreType.DMA((2, BLOCKS)),
            pltpu.SemaphoreType.REGULAR((8,)),
        ],
        compiler_params=pltpu.CompilerParams(
            collective_id=0, has_side_effects=True, vmem_limit_bytes=60 * 2**20
        ),
    )(
        lengths,
        *(
            array.reshape(halves)
            for array in (queries, key_vectors, value_vectors, gate_values, cotangent)
        ),
        norm_gain.reshape(1, width),
    )
    *grads, gain_total = pl.pallas_call(
        hand_over,
        out_shape=shapes,
        in_specs=[hbm] * 5,
        out_specs=(hbm,) * 5,
        scratch_shapes=[pltpu.VMEM(shape.shape, shape.dtype) for shape in shapes]
        + [pltpu.SemaphoreType.DMA((5,))] * 2,
        compiler_params=pltpu.CompilerParams(vmem_limit_bytes=60 * 2**20),
    )(*results)
    return *(array.reshape(row_count, width) for array in grads), gain_total.reshape(width)


def solution(mesh):
    rows = P(("dp", "ctx"), None)
    return jax.shard_map(
        body,
        mesh=mesh,
        in_specs=(rows,) * 5 + (P(), P("dp", None)),
        out_specs=(rows,) * 4 + (P(),),
        check_vma=False,
    )
```

```python
import math

import jax
import jax.numpy as jnp
from jax import lax
from jax.experimental import pallas as pl
from jax.experimental.pallas import tpu as pltpu
from jax.sharding import PartitionSpec as P

HEAD = 128
EPSILON = 1e-05
PEERS = 16
HEADS = 8
CHUNK = 64
HALF = PEERS * CHUNK
BLOCK = 256
PER_BLOCK = BLOCK // CHUNK
BLOCKS = HALF // BLOCK
PARTS = BLOCKS + 1
ROW = 4
ROWS_OF_PEERS = PEERS // ROW
EARLY_STEPS = BLOCKS // 2
STEPS = EARLY_STEPS + BLOCKS
SCALE = 1.0 / math.sqrt(HEAD)

QUERY_KEY, VALUE, ATT, GRAD, DQ, DKV, GAIN, GAIN_LAYER, GAIN_TOTAL = range(9)
KINDS = 9
MESH = pl.DeviceIdType.MESH


def contract(left, right, left_axis, right_axis):
    return lax.dot_general(
        left, right, (((left_axis,), (right_axis,)), ((), ())), preferred_element_type=jnp.float32
    )


def attention_kernel(
    groups,
    lengths_hbm,
    queries_hbm,
    keys_hbm,
    values_hbm,
    gates_hbm,
    cotangent_hbm,
    gain_hbm,
    output_hbm,
    grad_queries_hbm,
    grad_keys_hbm,
    grad_values_hbm,
    gain_total_hbm,
    lengths,
    own,
    gates,
    cotangent,
    gain,
    box,
    bounds,
    weights,
    slopes,
    att_sum,
    att_out,
    att_in,
    output,
    grad_out,
    grad_in,
    q_flipped,
    grad_flipped,
    dq_sum,
    sums,
    out_box,
    back,
    gain_slots,
    gain_total,
    local_sem,
    out_sem,
    send_sem,
    recv_sem,
    grad_sem,
    word_sem,
):
    me = lax.axis_index("ctx")
    group = lax.axis_index("dp")
    core = group % 2
    head = me // 2
    works = me % 2 == core
    place_z, layers = group // 2, groups // 2
    row, adder_place = me // ROW, 1 + core
    adds = me % ROW == adder_place
    partner = group + 1 - 2 * core
    others = slice(0, PEERS - 1)

    staged = [
        pltpu.make_async_copy(src, dst, local_sem.at[index])
        for index, (src, dst) in enumerate(
            (
                (queries_hbm, own.at[0]),
                (keys_hbm, own.at[1]),
                (values_hbm, own.at[2]),
                (lengths_hbm, lengths),
                (gates_hbm, gates),
                (cotangent_hbm, cotangent),
                (gain_hbm, gain),
            )
        )
    ]
    for copy in staged:
        copy.start()

    def columns(which):
        return pl.ds(pl.multiple_of(which * HEAD, HEAD), HEAD)

    def remote(src, dst, kind, half, target):
        return pltpu.make_async_remote_copy(
            src_ref=src,
            dst_ref=dst,
            send_sem=send_sem.at[kind, half],
            recv_sem=recv_sem.at[kind, half],
            device_id={"ctx": target},
            device_id_type=MESH,
        )

    def push(src, dst, kind, half, target):
        remote(src, dst, kind, half, target).start()

    def landed(ref, kind, half=0):
        remote(ref, ref, kind, half, me).wait_recv()

    def left(ref, kind, half=0):
        remote(ref, ref, kind, half, me).wait_send()

    def layer(distance):
        return 2 * lax.rem(place_z + distance + layers, layers) + core

    barrier = pltpu.get_barrier_semaphore()
    for turn in range(1, PEERS):
        pl.semaphore_signal(
            barrier, inc=1, device_id={"ctx": lax.rem(me + turn, PEERS)}, device_id_type=MESH
        )
    near = [{"dp": partner, "ctx": row * ROW + 2 - core}]
    if layers > 1:
        near += [{"dp": layer(1)}, {"dp": layer(-1)}]

    @pl.when(adds)
    def _():
        for peer in near:
            pl.semaphore_signal(barrier, inc=1, device_id=peer, device_id_type=MESH)

    for copy in staged[:4]:
        copy.wait()

    @pl.when(jnp.logical_not(adds))
    def _():
        pl.semaphore_wait(barrier, PEERS - 1)

    @pl.when(adds)
    def _():
        pl.semaphore_wait(barrier, PEERS - 1 + len(near))

    rounds = [1 << index for index in range(8) if 1 << index < layers // 2 + layers % 2]

    def row_mates(work):
        for turn in range(1, ROW):
            work(row * ROW + (me + turn) % ROW)

    def pass_words():
        pl.semaphore_signal(word_sem.at[6], inc=1, device_id=near[0], device_id_type=MESH)
        pl.semaphore_wait(word_sem.at[6], 1)
        row_mates(
            lambda peer: pl.semaphore_signal(
                word_sem.at[7], inc=1, device_id={"ctx": peer}, device_id_type=MESH
            )
        )
        for index, reach in enumerate(rounds):
            for distance in (reach, -reach):
                pl.semaphore_signal(
                    word_sem.at[index], inc=1, device_id={"dp": layer(distance)}, device_id_type=MESH
                )
            pl.semaphore_wait(word_sem.at[index], 2)

    def each_worker(work):
        def step(turn, carry):
            which = lax.rem(head + turn, HEADS)
            work(which, 2 * which + core)
            return carry

        lax.fori_loop(jnp.where(works, 1, 0), HEADS, step, 0)

    def by_count(work):
        @pl.when(works)
        def _():
            work(HEADS - 1)

        @pl.when(jnp.logical_not(works))
        def _():
            work(HEADS)

    for half in range(2):
        each_worker(
            lambda which, peer: push(
                own.at[:2, half, :, columns(which)], box.at[:2, half, me], QUERY_KEY, half, peer
            )
        )

    @pl.when(works)
    def _():
        box[:, :, me] = own[:, :, :, columns(head)]

    def queries_keys_left(count):
        for half in range(2):
            left(box.at[:2, half, :count], QUERY_KEY, half)

    by_count(queries_keys_left)
    each_worker(
        lambda which, peer: push(own.at[2, :, :, columns(which)], box.at[2, :, me], VALUE, 0, peer)
    )
    pl.when(adds)(pass_words)

    def times(half, block, shape, axis):
        place = lax.broadcasted_iota(jnp.int32, shape, axis)
        chunk, inner = place // CHUNK, place % CHUNK
        shard = block * PER_BLOCK + chunk
        return jnp.where(half == 0, shard, 2 * PEERS - 1 - shard) * CHUNK + inner

    def rows_of(which, half, block):
        start = pl.multiple_of(block * PER_BLOCK, PER_BLOCK)
        return box[which, half, pl.ds(start, PER_BLOCK)].reshape(BLOCK, HEAD)

    def chunks(block):
        return pl.ds(pl.multiple_of(block * PER_BLOCK, PER_BLOCK), PER_BLOCK)

    def place_of(half, block):
        return pl.ds(pl.multiple_of(half * HALF + block * BLOCK, BLOCK), BLOCK)

    def pair(step, part):
        early = step < EARLY_STEPS
        short = part <= step
        late_block = step - EARLY_STEPS
        reaches_back = part <= late_block
        q_half = jnp.where(early, 0, 1)
        q_block = jnp.where(early, jnp.where(short, step, BLOCKS - 1 - step), late_block)
        k_half = jnp.where(early | reaches_back, 0, 1)
        k_block = jnp.where(
            early,
            jnp.where(short, part, part - step - 1),
            jnp.where(reaches_back, BLOCKS - 1 - late_block + part, part - 1),
        )
        return q_half, q_block, k_half, k_block

    def for_blocks(step, work):
        @pl.when(step < EARLY_STEPS)
        def _():
            work(0, step)
            work(0, BLOCKS - 1 - step)

        @pl.when(step >= EARLY_STEPS)
        def _():
            work(1, step - EARLY_STEPS)

    def each_owner(block, work):
        for part in range(PER_BLOCK):
            shard = block * PER_BLOCK + part

            @pl.when(shard != me)
            def _():
                work(shard, False)

            @pl.when(shard == me)
            def _():
                work(shard, True)

    def deliver(src, dst, kind, half, shard, here):
        if here:
            dst[...] = src[...]
        else:
            push(src, dst, kind, half, shard)

    @pl.when(works)
    def _():
        ends = []
        total = 0
        for user in range(lengths.shape[1]):
            total = total + lengths[0, user]
            ends.append(total)

        def bounds_step(index, carry):
            half, block = index // BLOCKS, index % BLOCKS
            q_time = times(half, block, (BLOCK, HEAD), 0)
            first = jnp.zeros((BLOCK, HEAD), jnp.int32)
            for end in ends:
                first = jnp.where(q_time >= end, end, first)
            bounds[0, half, block] = first
            bounds[1, half, block] = q_time
            return carry

        lax.fori_loop(0, 2 * BLOCKS, bounds_step, 0)
        sums[...] = jnp.zeros(sums.shape, jnp.float32)
        dq_sum[...] = jnp.zeros(dq_sum.shape, jnp.float32)
        att_sum[...] = jnp.zeros(att_sum.shape, jnp.float32)
        landed(box.at[:2, 0, others], QUERY_KEY, 0)

        def score_step(step, carry):
            for part in range(PARTS):
                q_half, q_block, k_half, k_block = pair(step, part)
                k_time = times(k_half, k_block, (1, BLOCK), 1)
                first = jnp.tile(bounds[0, q_half, q_block], (1, BLOCK // HEAD))
                q_time = jnp.tile(bounds[1, q_half, q_block], (1, BLOCK // HEAD))
                raw = contract(rows_of(0, q_half, q_block), rows_of(1, k_half, k_block), 1, 1)
                scores = raw * SCALE
                live = (k_time >= first) & (k_time <= q_time)
                sigmoid = 0.5 * jnp.tanh(raw * (0.5 * SCALE)) + 0.5
                silu = scores * sigmoid
                slope = sigmoid * SCALE + silu * (SCALE - SCALE * sigmoid)
                weights[step, part] = jnp.where(live, silu, 0.0).astype(jnp.bfloat16)
                slopes[step, part] = jnp.where(live, slope, 0.0)
            return carry

        lax.fori_loop(0, EARLY_STEPS, score_step, 0)
        landed(box.at[:2, 1, others], QUERY_KEY, 1)
        lax.fori_loop(EARLY_STEPS, STEPS, score_step, 0)

    @pl.when(works)
    def _():
        landed(box.at[2, :, others], VALUE)

        def attend_step(step, carry):
            for part in range(PARTS):
                q_half, q_block, k_half, k_block = pair(step, part)
                att_sum[place_of(q_half, q_block), :] += contract(
                    weights[step, part], rows_of(2, k_half, k_block), 1, 0
                )

            def send(half, block):
                att_out[half, chunks(block)] = (
                    att_sum[place_of(half, block), :]
                    .astype(jnp.bfloat16)
                    .reshape(PER_BLOCK, CHUNK, HEAD)
                )
                each_owner(
                    block,
                    lambda shard, here: deliver(
                        att_out.at[half, shard],
                        att_in.at[half, :, columns(head)],
                        ATT,
                        half,
                        shard,
                        here,
                    ),
                )

            for_blocks(step, send)
            return carry

        lax.fori_loop(0, STEPS, attend_step, 0)

    def flip(matrix):
        return matrix.T

    @pl.when(works)
    def _():
        def flip_step(block, carry):
            for half in range(2):
                q_flipped[half, block] = flip(rows_of(0, half, block))
            return carry

        lax.fori_loop(0, BLOCKS, flip_step, 0)

    for copy in staged[4:]:
        copy.wait()
    gain_row = gain[...]

    def grad_copy(src, dst, half, block, target):
        return pltpu.make_async_remote_copy(
            src_ref=src,
            dst_ref=dst,
            send_sem=send_sem.at[GRAD, half],
            recv_sem=grad_sem.at[half, block],
            device_id={"ctx": target},
            device_id_type=MESH,
        )

    def grads_landed(half, block):
        @pl.when(me // PER_BLOCK == block)
        def _():
            rest = grad_in.at[half, : PER_BLOCK - 1]
            grad_copy(rest, rest, half, block, me).wait_recv()

        @pl.when(me // PER_BLOCK != block)
        def _():
            rest = grad_in.at[half, :PER_BLOCK]
            grad_copy(rest, rest, half, block, me).wait_recv()

    along = 2 * PEERS

    def gain_copy(slots, kind, target):
        return pltpu.make_async_remote_copy(
            src_ref=slots,
            dst_ref=slots,
            send_sem=send_sem.at[kind, 0],
            recv_sem=recv_sem.at[kind, 0],
            device_id=target,
            device_id_type=MESH,
        )

    def send_gain(gain_sum):
        mine = core * PEERS + me
        for which in range(HEADS):
            gain_slots[mine, which : which + 1, :] = gain_sum[:, which * HEAD : (which + 1) * HEAD]
        pl.when(jnp.logical_not(adds))(lambda: pl.semaphore_wait(word_sem.at[7], 1))
        for turn in range(ROWS_OF_PEERS):
            start = (row + turn) % ROWS_OF_PEERS * ROW
            if turn == 0:

                @pl.when(jnp.logical_not(adds))
                def _():
                    gain_copy(gain_slots.at[mine], GAIN, {"ctx": start + adder_place}).start()

            else:
                gain_copy(gain_slots.at[mine], GAIN, {"ctx": start + adder_place}).start()
            other = {"dp": partner, "ctx": start + 2 - core}
            gain_copy(gain_slots.at[mine], GAIN, other).start()

    def gain_over_groups():
        gain_copy(gain_slots.at[: 2 * PEERS - 1], GAIN, near[0]).wait_recv()
        mine = along + place_z
        gain_slots[mine] = jnp.sum(gain_slots[: 2 * PEERS], axis=0)

        def send(distance, carry):
            gain_copy(gain_slots.at[mine], GAIN_LAYER, {"dp": layer(distance)}).start()
            return carry

        if layers > 1:
            lax.fori_loop(1, layers, send, 0)
            gain_copy(gain_slots.at[along : along + layers - 1], GAIN_LAYER, near[0]).wait_recv()
        gain_total[...] = jnp.sum(gain_slots[along : along + layers], axis=0)
        row_mates(lambda peer: push(gain_total, gain_total, GAIN_TOTAL, 0, peer))

    def normalize_half(half, gain_before):
        by_count(lambda count: landed(att_in.at[half, :, : count * HEAD], ATT, half))

        def normalize(part, gain_sum):
            rows = pl.ds(pl.multiple_of(part * 32, 32), 32)
            attended = att_in[half, rows, :].astype(jnp.float32)
            centered = attended - jnp.mean(attended, axis=1, keepdims=True)
            variance = jnp.mean(centered * centered, axis=1, keepdims=True)
            inverse = lax.rsqrt(variance + EPSILON)
            normed = centered * inverse
            gate = gates[half, rows, :].astype(jnp.float32)
            grad = cotangent[half, rows, :].astype(jnp.float32)
            scaled = gate * gain_row
            output[half, rows, :] = (normed * scaled).astype(jnp.bfloat16)
            gain_sum = gain_sum + jnp.sum(normed * grad * gate, axis=0, keepdims=True)
            grad = grad * scaled
            grad_out[half, rows, :] = (
                (
                    grad
                    - jnp.mean(grad, axis=1, keepdims=True)
                    - normed * jnp.mean(grad * normed, axis=1, keepdims=True)
                )
                * inverse
            ).astype(jnp.bfloat16)
            return gain_sum

        gain_sum = lax.fori_loop(
            0, CHUNK // 32, normalize, gain_before
        )
        if half == 1:
            send_gain(gain_sum)
        each_worker(
            lambda which, peer: grad_copy(
                grad_out.at[half, :, columns(which)], grad_in.at[half, me], half, me // PER_BLOCK, peer
            ).start()
        )

        @pl.when(works)
        def _():
            grad_in[half, me] = grad_out[half, :, columns(head)]

        return gain_sum

    normalize_half(1, normalize_half(0, jnp.zeros((1, gain.shape[1]), jnp.float32)))
    output_copy = pltpu.make_async_copy(output, output_hbm, out_sem.at[0])
    output_copy.start()

    def finish(half, block):
        for index in range(2):
            out_box[1 + index, half, chunks(block)] = (
                sums[index, :, place_of(half, block)]
                .astype(jnp.bfloat16)
                .T
                .reshape(PER_BLOCK, CHUNK, HEAD)
            )

    def backward_step(step, carry):
        def prepare(half, block):
            grads_landed(half, block)
            grad_flipped[half, block] = flip(grad_in[half, chunks(block)].reshape(BLOCK, HEAD))

        for_blocks(step, prepare)
        @pl.when(step < EARLY_STEPS)
        def _():
            for part in range(PARTS):
                q_half, q_block, k_half, k_block = pair(step, part)
                grad = grad_in[q_half, chunks(q_block)].reshape(BLOCK, HEAD)
                place = place_of(k_half, k_block)
                grad_weights = contract(grad, rows_of(2, k_half, k_block), 1, 1)
                grad_scores = (grad_weights * slopes[step, part]).astype(jnp.bfloat16)
                sums[0, :, place] += contract(q_flipped[q_half, q_block], grad_scores, 1, 0)
                sums[1, :, place] += contract(grad_flipped[q_half, q_block], weights[step, part], 1, 0)
                dq_sum[place_of(q_half, q_block), :] += contract(
                    grad_scores, rows_of(1, k_half, k_block), 1, 0
                )

        @pl.when(step >= EARLY_STEPS)
        def _():
            q_block = step - EARLY_STEPS
            grad = grad_in[1, chunks(q_block)].reshape(BLOCK, HEAD)
            met = [pair(step, part)[2:] for part in range(PARTS)]
            window = [
                jnp.concatenate([rows_of(which, *each) for each in met], axis=0) for which in (1, 2)
            ]
            grad_weights = contract(grad, window[1], 1, 1)
            slope = jnp.concatenate([slopes[step, part] for part in range(PARTS)], axis=1)
            weight = jnp.concatenate([weights[step, part] for part in range(PARTS)], axis=1)
            grad_scores = (grad_weights * slope).astype(jnp.bfloat16)
            dq_sum[place_of(1, q_block), :] = contract(grad_scores, window[0], 1, 0)
            dk = contract(q_flipped[1, q_block], grad_scores, 1, 0)
            dv = contract(grad_flipped[1, q_block], weight, 1, 0)
            for part, each in enumerate(met):
                cols = slice(part * BLOCK, (part + 1) * BLOCK)
                sums[0, :, place_of(*each)] += dk[:, cols]
                sums[1, :, place_of(*each)] += dv[:, cols]

        def send_queries(half, block):
            out_box[0, half, chunks(block)] = (
                dq_sum[place_of(half, block), :]
                .astype(jnp.bfloat16)
                .reshape(PER_BLOCK, CHUNK, HEAD)
            )
            if half == 1:
                finish(1, block)
            count = 1 + 2 * half
            each_owner(
                block,
                lambda shard, here: deliver(
                    out_box.at[:count, half, shard],
                    back.at[:count, half, :, columns(head)],
                    DQ,
                    half,
                    shard,
                    here,
                ),
            )

        for_blocks(step, send_queries)
        return carry

    pl.when(adds)(gain_over_groups)

    @pl.when(works)
    def _():
        lax.fori_loop(0, STEPS, backward_step, 0)

        def finish_early(block, carry):
            finish(0, block)
            each_owner(
                block,
                lambda shard, here: deliver(
                    out_box.at[1:, 0, shard],
                    back.at[1:, 0, :, columns(head)],
                    DKV,
                    0,
                    shard,
                    here,
                ),
            )
            return carry

        lax.fori_loop(0, BLOCKS, finish_early, 0)

    def result_copy(index, half, slot):
        result = (grad_queries_hbm, grad_keys_hbm, grad_values_hbm)[index]
        return pltpu.make_async_copy(back.at[index, half], result.at[half], out_sem.at[slot])

    results = [result_copy(0, 0, 1), result_copy(0, 1, 2), result_copy(1, 1, 3), result_copy(2, 1, 4)]
    by_count(lambda count: landed(back.at[0, 0, :, : count * HEAD], DQ, 0))
    results[0].start()
    by_count(lambda count: landed(back.at[:, 1, :, : count * HEAD], DQ, 1))
    for copy in results[1:]:
        copy.start()
    by_count(lambda count: landed(back.at[1:, 0, :, : count * HEAD], DKV))
    results += [result_copy(1, 0, 5), result_copy(2, 0, 6)]
    for copy in results[-2:]:
        copy.start()
    pl.when(jnp.logical_not(adds))(lambda: landed(gain_total, GAIN_TOTAL))
    results.append(pltpu.make_async_copy(gain_total, gain_total_hbm, out_sem.at[7]))
    results[-1].start()

    @pl.when(works)
    def _():
        for half in range(2):
            left(att_out.at[half, others], ATT, half)
        left(out_box.at[0, 0, others], DQ, 0)
        left(out_box.at[:, 1, others], DQ, 1)
        left(out_box.at[1:, 0, others], DKV)

    def inputs_left(count):
        left(box.at[2, :, :count], VALUE)
        for half in range(2):
            left(grad_in.at[half, :count], GRAD, half)

    by_count(inputs_left)

    @pl.when(jnp.logical_not(adds))
    def _():
        left(gain_slots.at[: 2 * ROWS_OF_PEERS], GAIN)

    @pl.when(adds)
    def _():
        left(gain_slots.at[: 2 * ROWS_OF_PEERS - 1], GAIN)
        if layers > 1:
            gain_copy(gain_slots.at[along : along + layers - 1], GAIN_LAYER, near[0]).wait_send()
        left(gain_slots.at[: ROW - 1], GAIN_TOTAL)

    output_copy.wait()
    for copy in results:
        copy.wait()


def hand_over(*refs):
    count = (len(refs) - 2) // 3
    sources, results, held = refs[:count], refs[count : 2 * count], refs[2 * count : 3 * count]
    into = [
        pltpu.make_async_copy(src, dst, refs[-2].at[index])
        for index, (src, dst) in enumerate(zip(sources, held))
    ]
    out = [
        pltpu.make_async_copy(src, dst, refs[-1].at[index])
        for index, (src, dst) in enumerate(zip(held, results))
    ]
    for copy in into:
        copy.start()
    for copy, after in zip(into, out):
        copy.wait()
        after.start()
    for copy in out:
        copy.wait()


def body(queries, key_vectors, value_vectors, gate_values, cotangent, norm_gain, lengths):
    row_count, width = queries.shape
    groups = lax.axis_size("dp")
    halves = (2, CHUNK, width)
    wide = jax.ShapeDtypeStruct(halves, jnp.bfloat16)
    hbm = pl.BlockSpec(memory_space=pltpu.HBM)
    boxes = (2, PEERS, CHUNK, HEAD)

    def kernel(*refs):
        attention_kernel(groups, *refs)

    shapes = (wide, wide, wide, wide, jax.ShapeDtypeStruct((HEADS, HEAD), jnp.float32))
    results = pl.pallas_call(
        kernel,
        out_shape=shapes,
        in_specs=[hbm] * 7,
        out_specs=(hbm,) * 5,
        scratch_shapes=[
            pltpu.SMEM(lengths.shape, jnp.int32),
            pltpu.VMEM((3,) + halves, jnp.bfloat16),
            pltpu.VMEM(halves, jnp.bfloat16),
            pltpu.VMEM(halves, jnp.bfloat16),
            pltpu.VMEM((1, width), jnp.float32),
            pltpu.VMEM((3,) + boxes, jnp.bfloat16),
            pltpu.VMEM((2, 2, BLOCKS, BLOCK, HEAD), jnp.int32),
            pltpu.VMEM((STEPS, PARTS, BLOCK, BLOCK), jnp.bfloat16),
            pltpu.VMEM((STEPS, PARTS, BLOCK, BLOCK), jnp.float32),
            pltpu.VMEM((2 * HALF, HEAD), jnp.float32),
            pltpu.VMEM(boxes, jnp.bfloat16),
            pltpu.VMEM(halves, jnp.bfloat16),
            pltpu.VMEM(halves, jnp.bfloat16),
            pltpu.VMEM(halves, jnp.bfloat16),
            pltpu.VMEM(boxes, jnp.bfloat16),
            pltpu.VMEM((2, BLOCKS, HEAD, BLOCK), jnp.bfloat16),
            pltpu.VMEM((2, BLOCKS, HEAD, BLOCK), jnp.bfloat16),
            pltpu.VMEM((2 * HALF, HEAD), jnp.float32),
            pltpu.VMEM((2, HEAD, 2 * HALF), jnp.float32),
            pltpu.VMEM((3,) + boxes, jnp.bfloat16),
            pltpu.VMEM((3,) + halves, jnp.bfloat16),
            pltpu.VMEM((2 * PEERS + groups // 2, HEADS, HEAD), jnp.float32),
            pltpu.VMEM((HEADS, HEAD), jnp.float32),
            pltpu.SemaphoreType.DMA((7,)),
            pltpu.SemaphoreType.DMA((8,)),
            pltpu.SemaphoreType.DMA((KINDS, 2)),
            pltpu.SemaphoreType.DMA((KINDS, 2)),
            pltpu.SemaphoreType.DMA((2, BLOCKS)),
            pltpu.SemaphoreType.REGULAR((8,)),
        ],
        compiler_params=pltpu.CompilerParams(
            collective_id=0, has_side_effects=True, vmem_limit_bytes=60 * 2**20
        ),
    )(
        lengths,
        *(
            array.reshape(halves)
            for array in (queries, key_vectors, value_vectors, gate_values, cotangent)
        ),
        norm_gain.reshape(1, width),
    )
    *grads, gain_total = pl.pallas_call(
        hand_over,
        out_shape=shapes,
        in_specs=[hbm] * 5,
        out_specs=(hbm,) * 5,
        scratch_shapes=[pltpu.VMEM(shape.shape, shape.dtype) for shape in shapes]
        + [pltpu.SemaphoreType.DMA((5,))] * 2,
        compiler_params=pltpu.CompilerParams(vmem_limit_bytes=60 * 2**20),
    )(*results)
    return *(array.reshape(row_count, width) for array in grads), gain_total.reshape(width)


def solution(mesh):
    rows = P(("dp", "ctx"), None)
    return jax.shard_map(
        body,
        mesh=mesh,
        in_specs=(rows,) * 5 + (P(), P("dp", None)),
        out_specs=(rows,) * 4 + (P(),),
        check_vma=False,
    )
```

```python
import math

import jax
import jax.numpy as jnp
from jax import lax
from jax.experimental import pallas as pl
from jax.experimental.pallas import tpu as pltpu
from jax.sharding import PartitionSpec as P

HEAD = 128
EPSILON = 1e-05
PEERS = 16
HEADS = 8
CHUNK = 64
HALF = PEERS * CHUNK
BLOCK = 256
PER_BLOCK = BLOCK // CHUNK
BLOCKS = HALF // BLOCK
PARTS = BLOCKS + 1
ROW = 4
ROWS_OF_PEERS = PEERS // ROW
EARLY_STEPS = BLOCKS // 2
STEPS = EARLY_STEPS + BLOCKS
SCALE = 1.0 / math.sqrt(HEAD)

QUERY_KEY, VALUE, ATT, GRAD, DQ, DKV, GAIN, GAIN_LAYER, GAIN_TOTAL = range(9)
KINDS = 9
MESH = pl.DeviceIdType.MESH


def contract(left, right, left_axis, right_axis):
    return lax.dot_general(
        left, right, (((left_axis,), (right_axis,)), ((), ())), preferred_element_type=jnp.float32
    )


def attention_kernel(
    groups,
    lengths_hbm,
    queries_hbm,
    keys_hbm,
    values_hbm,
    gates_hbm,
    cotangent_hbm,
    gain_hbm,
    output_hbm,
    grad_queries_hbm,
    grad_keys_hbm,
    grad_values_hbm,
    gain_total_hbm,
    lengths,
    own,
    gates,
    cotangent,
    gain,
    box,
    bounds,
    weights,
    slopes,
    att_sum,
    att_out,
    att_in,
    output,
    grad_out,
    grad_in,
    q_flipped,
    grad_flipped,
    dq_sum,
    sums,
    out_box,
    back,
    gain_slots,
    gain_total,
    local_sem,
    out_sem,
    send_sem,
    recv_sem,
    grad_sem,
    word_sem,
):
    me = lax.axis_index("ctx")
    group = lax.axis_index("dp")
    core = group % 2
    head = me // 2
    works = me % 2 == core
    place_z, layers = group // 2, groups // 2
    row, adder_place = me // ROW, 1 + core
    adds = me % ROW == adder_place
    partner = group + 1 - 2 * core
    others = slice(0, PEERS - 1)

    staged = [
        pltpu.make_async_copy(src, dst, local_sem.at[index])
        for index, (src, dst) in enumerate(
            (
                (queries_hbm, own.at[0]),
                (keys_hbm, own.at[1]),
                (values_hbm, own.at[2]),
                (lengths_hbm, lengths),
                (gates_hbm, gates),
                (cotangent_hbm, cotangent),
                (gain_hbm, gain),
            )
        )
    ]
    for copy in staged:
        copy.start()

    def columns(which):
        return pl.ds(pl.multiple_of(which * HEAD, HEAD), HEAD)

    def remote(src, dst, kind, half, target):
        return pltpu.make_async_remote_copy(
            src_ref=src,
            dst_ref=dst,
            send_sem=send_sem.at[kind, half],
            recv_sem=recv_sem.at[kind, half],
            device_id={"ctx": target},
            device_id_type=MESH,
        )

    def push(src, dst, kind, half, target):
        remote(src, dst, kind, half, target).start()

    def landed(ref, kind, half=0):
        remote(ref, ref, kind, half, me).wait_recv()

    def left(ref, kind, half=0):
        remote(ref, ref, kind, half, me).wait_send()

    def layer(distance):
        return 2 * lax.rem(place_z + distance + layers, layers) + core

    barrier = pltpu.get_barrier_semaphore()
    for turn in range(1, PEERS):
        pl.semaphore_signal(
            barrier, inc=1, device_id={"ctx": lax.rem(me + turn, PEERS)}, device_id_type=MESH
        )
    near = [{"dp": partner, "ctx": row * ROW + 2 - core}]
    if layers > 1:
        near += [{"dp": layer(1)}, {"dp": layer(-1)}]

    @pl.when(adds)
    def _():
        for peer in near:
            pl.semaphore_signal(barrier, inc=1, device_id=peer, device_id_type=MESH)

    for copy in staged[:4]:
        copy.wait()

    @pl.when(jnp.logical_not(adds))
    def _():
        pl.semaphore_wait(barrier, PEERS - 1)

    @pl.when(adds)
    def _():
        pl.semaphore_wait(barrier, PEERS - 1 + len(near))

    rounds = [1 << index for index in range(8) if 1 << index < layers // 2 + layers % 2]

    def row_mates(work):
        for turn in range(1, ROW):
            work(row * ROW + (me + turn) % ROW)

    def pass_words():
        pl.semaphore_signal(word_sem.at[6], inc=1, device_id=near[0], device_id_type=MESH)
        pl.semaphore_wait(word_sem.at[6], 1)
        row_mates(
            lambda peer: pl.semaphore_signal(
                word_sem.at[7], inc=1, device_id={"ctx": peer}, device_id_type=MESH
            )
        )
        for index, reach in enumerate(rounds):
            for distance in (reach, -reach):
                pl.semaphore_signal(
                    word_sem.at[index], inc=1, device_id={"dp": layer(distance)}, device_id_type=MESH
                )
            pl.semaphore_wait(word_sem.at[index], 2)

    def each_worker(work):
        def step(turn, carry):
            which = lax.rem(head + turn, HEADS)
            work(which, 2 * which + core)
            return carry

        lax.fori_loop(jnp.where(works, 1, 0), HEADS, step, 0)

    def by_count(work):
        @pl.when(works)
        def _():
            work(HEADS - 1)

        @pl.when(jnp.logical_not(works))
        def _():
            work(HEADS)

    for half in range(2):
        each_worker(
            lambda which, peer: push(
                own.at[:2, half, :, columns(which)], box.at[:2, half, me], QUERY_KEY, half, peer
            )
        )

    @pl.when(works)
    def _():
        box[:, :, me] = own[:, :, :, columns(head)]

    def queries_keys_left(count):
        for half in range(2):
            left(box.at[:2, half, :count], QUERY_KEY, half)

    by_count(queries_keys_left)
    each_worker(
        lambda which, peer: push(own.at[2, :, :, columns(which)], box.at[2, :, me], VALUE, 0, peer)
    )
    pl.when(adds)(pass_words)

    def times(half, block, shape, axis):
        place = lax.broadcasted_iota(jnp.int32, shape, axis)
        chunk, inner = place // CHUNK, place % CHUNK
        shard = block * PER_BLOCK + chunk
        return jnp.where(half == 0, shard, 2 * PEERS - 1 - shard) * CHUNK + inner

    def rows_of(which, half, block):
        start = pl.multiple_of(block * PER_BLOCK, PER_BLOCK)
        return box[which, half, pl.ds(start, PER_BLOCK)].reshape(BLOCK, HEAD)

    def chunks(block):
        return pl.ds(pl.multiple_of(block * PER_BLOCK, PER_BLOCK), PER_BLOCK)

    def place_of(half, block):
        return pl.ds(pl.multiple_of(half * HALF + block * BLOCK, BLOCK), BLOCK)

    def pair(step, part):
        early = step < EARLY_STEPS
        short = part <= step
        late_block = step - EARLY_STEPS
        reaches_back = part <= late_block
        q_half = jnp.where(early, 0, 1)
        q_block = jnp.where(early, jnp.where(short, step, BLOCKS - 1 - step), late_block)
        k_half = jnp.where(early | reaches_back, 0, 1)
        k_block = jnp.where(
            early,
            jnp.where(short, part, part - step - 1),
            jnp.where(reaches_back, BLOCKS - 1 - late_block + part, part - 1),
        )
        return q_half, q_block, k_half, k_block

    def for_blocks(step, work):
        @pl.when(step < EARLY_STEPS)
        def _():
            work(0, step)
            work(0, BLOCKS - 1 - step)

        @pl.when(step >= EARLY_STEPS)
        def _():
            work(1, step - EARLY_STEPS)

    def each_owner(block, work):
        for part in range(PER_BLOCK):
            shard = block * PER_BLOCK + part

            @pl.when(shard != me)
            def _():
                work(shard, False)

            @pl.when(shard == me)
            def _():
                work(shard, True)

    def deliver(src, dst, kind, half, shard, here):
        if here:
            dst[...] = src[...]
        else:
            push(src, dst, kind, half, shard)

    @pl.when(works)
    def _():
        ends = []
        total = 0
        for user in range(lengths.shape[1]):
            total = total + lengths[0, user]
            ends.append(total)

        def bounds_step(index, carry):
            half, block = index // BLOCKS, index % BLOCKS
            q_time = times(half, block, (BLOCK, HEAD), 0)
            first = jnp.zeros((BLOCK, HEAD), jnp.int32)
            for end in ends:
                first = jnp.where(q_time >= end, end, first)
            bounds[0, half, block] = first
            bounds[1, half, block] = q_time
            return carry

        lax.fori_loop(0, 2 * BLOCKS, bounds_step, 0)
        sums[...] = jnp.zeros(sums.shape, jnp.float32)
        dq_sum[...] = jnp.zeros(dq_sum.shape, jnp.float32)
        att_sum[...] = jnp.zeros(att_sum.shape, jnp.float32)
        landed(box.at[:2, 0, others], QUERY_KEY, 0)

        def score_step(step, carry):
            for part in range(PARTS):
                q_half, q_block, k_half, k_block = pair(step, part)
                k_time = times(k_half, k_block, (1, BLOCK), 1)
                first = jnp.tile(bounds[0, q_half, q_block], (1, BLOCK // HEAD))
                q_time = jnp.tile(bounds[1, q_half, q_block], (1, BLOCK // HEAD))
                raw = contract(rows_of(0, q_half, q_block), rows_of(1, k_half, k_block), 1, 1)
                scores = raw * SCALE
                live = (k_time >= first) & (k_time <= q_time)
                sigmoid = 0.5 * jnp.tanh(raw * (0.5 * SCALE)) + 0.5
                silu = scores * sigmoid
                slope = sigmoid * SCALE + silu * (SCALE - SCALE * sigmoid)
                weights[step, part] = jnp.where(live, silu, 0.0).astype(jnp.bfloat16)
                slopes[step, part] = jnp.where(live, slope, 0.0)
            return carry

        lax.fori_loop(0, EARLY_STEPS, score_step, 0)
        landed(box.at[:2, 1, others], QUERY_KEY, 1)
        lax.fori_loop(EARLY_STEPS, STEPS, score_step, 0)

    @pl.when(works)
    def _():
        landed(box.at[2, :, others], VALUE)

        def attend_step(step, carry):
            for part in range(PARTS):
                q_half, q_block, k_half, k_block = pair(step, part)
                att_sum[place_of(q_half, q_block), :] += contract(
                    weights[step, part], rows_of(2, k_half, k_block), 1, 0
                )

            def send(half, block):
                att_out[half, chunks(block)] = (
                    att_sum[place_of(half, block), :]
                    .astype(jnp.bfloat16)
                    .reshape(PER_BLOCK, CHUNK, HEAD)
                )
                each_owner(
                    block,
                    lambda shard, here: deliver(
                        att_out.at[half, shard],
                        att_in.at[half, :, columns(head)],
                        ATT,
                        half,
                        shard,
                        here,
                    ),
                )

            for_blocks(step, send)
            return carry

        lax.fori_loop(0, STEPS, attend_step, 0)

    def flip(matrix):
        return matrix.T

    for copy in staged[4:]:
        copy.wait()
    gain_row = gain[...]

    def grad_copy(src, dst, half, block, target):
        return pltpu.make_async_remote_copy(
            src_ref=src,
            dst_ref=dst,
            send_sem=send_sem.at[GRAD, half],
            recv_sem=grad_sem.at[half, block],
            device_id={"ctx": target},
            device_id_type=MESH,
        )

    def grads_landed(half, block):
        @pl.when(me // PER_BLOCK == block)
        def _():
            rest = grad_in.at[half, : PER_BLOCK - 1]
            grad_copy(rest, rest, half, block, me).wait_recv()

        @pl.when(me // PER_BLOCK != block)
        def _():
            rest = grad_in.at[half, :PER_BLOCK]
            grad_copy(rest, rest, half, block, me).wait_recv()

    along = 2 * PEERS

    def gain_copy(slots, kind, target):
        return pltpu.make_async_remote_copy(
            src_ref=slots,
            dst_ref=slots,
            send_sem=send_sem.at[kind, 0],
            recv_sem=recv_sem.at[kind, 0],
            device_id=target,
            device_id_type=MESH,
        )

    def send_gain(gain_sum):
        mine = core * PEERS + me
        for which in range(HEADS):
            gain_slots[mine, which : which + 1, :] = gain_sum[:, which * HEAD : (which + 1) * HEAD]
        pl.when(jnp.logical_not(adds))(lambda: pl.semaphore_wait(word_sem.at[7], 1))
        for turn in range(ROWS_OF_PEERS):
            start = (row + turn) % ROWS_OF_PEERS * ROW
            if turn == 0:

                @pl.when(jnp.logical_not(adds))
                def _():
                    gain_copy(gain_slots.at[mine], GAIN, {"ctx": start + adder_place}).start()

            else:
                gain_copy(gain_slots.at[mine], GAIN, {"ctx": start + adder_place}).start()
            other = {"dp": partner, "ctx": start + 2 - core}
            gain_copy(gain_slots.at[mine], GAIN, other).start()

    def gain_over_groups():
        gain_copy(gain_slots.at[: 2 * PEERS - 1], GAIN, near[0]).wait_recv()
        mine = along + place_z
        gain_slots[mine] = jnp.sum(gain_slots[: 2 * PEERS], axis=0)

        def send(distance, carry):
            gain_copy(gain_slots.at[mine], GAIN_LAYER, {"dp": layer(distance)}).start()
            return carry

        if layers > 1:
            lax.fori_loop(1, layers, send, 0)
            gain_copy(gain_slots.at[along : along + layers - 1], GAIN_LAYER, near[0]).wait_recv()
        gain_total[...] = jnp.sum(gain_slots[along : along + layers], axis=0)
        row_mates(lambda peer: push(gain_total, gain_total, GAIN_TOTAL, 0, peer))

    def normalize_half(half, gain_before):
        by_count(lambda count: landed(att_in.at[half, :, : count * HEAD], ATT, half))

        def normalize(part, gain_sum):
            rows = pl.ds(pl.multiple_of(part * 32, 32), 32)
            attended = att_in[half, rows, :].astype(jnp.float32)
            centered = attended - jnp.mean(attended, axis=1, keepdims=True)
            variance = jnp.mean(centered * centered, axis=1, keepdims=True)
            inverse = lax.rsqrt(variance + EPSILON)
            normed = centered * inverse
            gate = gates[half, rows, :].astype(jnp.float32)
            grad = cotangent[half, rows, :].astype(jnp.float32)
            scaled = gate * gain_row
            output[half, rows, :] = (normed * scaled).astype(jnp.bfloat16)
            gain_sum = gain_sum + jnp.sum(normed * grad * gate, axis=0, keepdims=True)
            grad = grad * scaled
            grad_out[half, rows, :] = (
                (
                    grad
                    - jnp.mean(grad, axis=1, keepdims=True)
                    - normed * jnp.mean(grad * normed, axis=1, keepdims=True)
                )
                * inverse
            ).astype(jnp.bfloat16)
            return gain_sum

        gain_sum = lax.fori_loop(
            0, CHUNK // 32, normalize, gain_before
        )
        if half == 1:
            send_gain(gain_sum)
        each_worker(
            lambda which, peer: grad_copy(
                grad_out.at[half, :, columns(which)], grad_in.at[half, me], half, me // PER_BLOCK, peer
            ).start()
        )

        @pl.when(works)
        def _():
            grad_in[half, me] = grad_out[half, :, columns(head)]

        return gain_sum

    gain_early = normalize_half(0, jnp.zeros((1, gain.shape[1]), jnp.float32))
    @pl.when(works)
    def _():
        def flip_step(block, carry):
            for half in range(2):
                q_flipped[half, block] = flip(rows_of(0, half, block))
            return carry

        lax.fori_loop(0, BLOCKS, flip_step, 0)

    normalize_half(1, gain_early)
    output_copy = pltpu.make_async_copy(output, output_hbm, out_sem.at[0])
    output_copy.start()

    def finish(half, block):
        for index in range(2):
            out_box[1 + index, half, chunks(block)] = (
                sums[index, :, place_of(half, block)]
                .astype(jnp.bfloat16)
                .T
                .reshape(PER_BLOCK, CHUNK, HEAD)
            )

    def backward_step(step, carry):
        def prepare(half, block):
            grads_landed(half, block)
            grad_flipped[half, block] = flip(grad_in[half, chunks(block)].reshape(BLOCK, HEAD))

        for_blocks(step, prepare)
        @pl.when(step < EARLY_STEPS)
        def _():
            for part in range(PARTS):
                q_half, q_block, k_half, k_block = pair(step, part)
                grad = grad_in[q_half, chunks(q_block)].reshape(BLOCK, HEAD)
                place = place_of(k_half, k_block)
                grad_weights = contract(grad, rows_of(2, k_half, k_block), 1, 1)
                grad_scores = (grad_weights * slopes[step, part]).astype(jnp.bfloat16)
                sums[0, :, place] += contract(q_flipped[q_half, q_block], grad_scores, 1, 0)
                sums[1, :, place] += contract(grad_flipped[q_half, q_block], weights[step, part], 1, 0)
                dq_sum[place_of(q_half, q_block), :] += contract(
                    grad_scores, rows_of(1, k_half, k_block), 1, 0
                )

        @pl.when(step >= EARLY_STEPS)
        def _():
            q_block = step - EARLY_STEPS
            grad = grad_in[1, chunks(q_block)].reshape(BLOCK, HEAD)
            met = [pair(step, part)[2:] for part in range(PARTS)]
            window = [
                jnp.concatenate([rows_of(which, *each) for each in met], axis=0) for which in (1, 2)
            ]
            grad_weights = contract(grad, window[1], 1, 1)
            slope = jnp.concatenate([slopes[step, part] for part in range(PARTS)], axis=1)
            weight = jnp.concatenate([weights[step, part] for part in range(PARTS)], axis=1)
            grad_scores = (grad_weights * slope).astype(jnp.bfloat16)
            dq_sum[place_of(1, q_block), :] = contract(grad_scores, window[0], 1, 0)
            dk = contract(q_flipped[1, q_block], grad_scores, 1, 0)
            dv = contract(grad_flipped[1, q_block], weight, 1, 0)
            for part, each in enumerate(met):
                cols = slice(part * BLOCK, (part + 1) * BLOCK)
                sums[0, :, place_of(*each)] += dk[:, cols]
                sums[1, :, place_of(*each)] += dv[:, cols]

        def send_queries(half, block):
            out_box[0, half, chunks(block)] = (
                dq_sum[place_of(half, block), :]
                .astype(jnp.bfloat16)
                .reshape(PER_BLOCK, CHUNK, HEAD)
            )
            if half == 1:
                finish(1, block)
            count = 1 + 2 * half
            each_owner(
                block,
                lambda shard, here: deliver(
                    out_box.at[:count, half, shard],
                    back.at[:count, half, :, columns(head)],
                    DQ,
                    half,
                    shard,
                    here,
                ),
            )

        for_blocks(step, send_queries)
        return carry

    pl.when(adds)(gain_over_groups)

    @pl.when(works)
    def _():
        lax.fori_loop(0, STEPS, backward_step, 0)

        def finish_early(block, carry):
            finish(0, block)
            each_owner(
                block,
                lambda shard, here: deliver(
                    out_box.at[1:, 0, shard],
                    back.at[1:, 0, :, columns(head)],
                    DKV,
                    0,
                    shard,
                    here,
                ),
            )
            return carry

        lax.fori_loop(0, BLOCKS, finish_early, 0)

    def result_copy(index, half, slot):
        result = (grad_queries_hbm, grad_keys_hbm, grad_values_hbm)[index]
        return pltpu.make_async_copy(back.at[index, half], result.at[half], out_sem.at[slot])

    results = [result_copy(0, 0, 1), result_copy(0, 1, 2), result_copy(1, 1, 3), result_copy(2, 1, 4)]
    by_count(lambda count: landed(back.at[0, 0, :, : count * HEAD], DQ, 0))
    results[0].start()
    by_count(lambda count: landed(back.at[:, 1, :, : count * HEAD], DQ, 1))
    for copy in results[1:]:
        copy.start()
    by_count(lambda count: landed(back.at[1:, 0, :, : count * HEAD], DKV))
    results += [result_copy(1, 0, 5), result_copy(2, 0, 6)]
    for copy in results[-2:]:
        copy.start()
    pl.when(jnp.logical_not(adds))(lambda: landed(gain_total, GAIN_TOTAL))
    results.append(pltpu.make_async_copy(gain_total, gain_total_hbm, out_sem.at[7]))
    results[-1].start()

    @pl.when(works)
    def _():
        for half in range(2):
            left(att_out.at[half, others], ATT, half)
        left(out_box.at[0, 0, others], DQ, 0)
        left(out_box.at[:, 1, others], DQ, 1)
        left(out_box.at[1:, 0, others], DKV)

    def inputs_left(count):
        left(box.at[2, :, :count], VALUE)
        for half in range(2):
            left(grad_in.at[half, :count], GRAD, half)

    by_count(inputs_left)

    @pl.when(jnp.logical_not(adds))
    def _():
        left(gain_slots.at[: 2 * ROWS_OF_PEERS], GAIN)

    @pl.when(adds)
    def _():
        left(gain_slots.at[: 2 * ROWS_OF_PEERS - 1], GAIN)
        if layers > 1:
            gain_copy(gain_slots.at[along : along + layers - 1], GAIN_LAYER, near[0]).wait_send()
        left(gain_slots.at[: ROW - 1], GAIN_TOTAL)

    output_copy.wait()
    for copy in results:
        copy.wait()


def hand_over(*refs):
    count = (len(refs) - 2) // 3
    sources, results, held = refs[:count], refs[count : 2 * count], refs[2 * count : 3 * count]
    into = [
        pltpu.make_async_copy(src, dst, refs[-2].at[index])
        for index, (src, dst) in enumerate(zip(sources, held))
    ]
    out = [
        pltpu.make_async_copy(src, dst, refs[-1].at[index])
        for index, (src, dst) in enumerate(zip(held, results))
    ]
    for copy in into:
        copy.start()
    for copy, after in zip(into, out):
        copy.wait()
        after.start()
    for copy in out:
        copy.wait()


def body(queries, key_vectors, value_vectors, gate_values, cotangent, norm_gain, lengths):
    row_count, width = queries.shape
    groups = lax.axis_size("dp")
    halves = (2, CHUNK, width)
    wide = jax.ShapeDtypeStruct(halves, jnp.bfloat16)
    hbm = pl.BlockSpec(memory_space=pltpu.HBM)
    boxes = (2, PEERS, CHUNK, HEAD)

    def kernel(*refs):
        attention_kernel(groups, *refs)

    shapes = (wide, wide, wide, wide, jax.ShapeDtypeStruct((HEADS, HEAD), jnp.float32))
    results = pl.pallas_call(
        kernel,
        out_shape=shapes,
        in_specs=[hbm] * 7,
        out_specs=(hbm,) * 5,
        scratch_shapes=[
            pltpu.SMEM(lengths.shape, jnp.int32),
            pltpu.VMEM((3,) + halves, jnp.bfloat16),
            pltpu.VMEM(halves, jnp.bfloat16),
            pltpu.VMEM(halves, jnp.bfloat16),
            pltpu.VMEM((1, width), jnp.float32),
            pltpu.VMEM((3,) + boxes, jnp.bfloat16),
            pltpu.VMEM((2, 2, BLOCKS, BLOCK, HEAD), jnp.int32),
            pltpu.VMEM((STEPS, PARTS, BLOCK, BLOCK), jnp.bfloat16),
            pltpu.VMEM((STEPS, PARTS, BLOCK, BLOCK), jnp.float32),
            pltpu.VMEM((2 * HALF, HEAD), jnp.float32),
            pltpu.VMEM(boxes, jnp.bfloat16),
            pltpu.VMEM(halves, jnp.bfloat16),
            pltpu.VMEM(halves, jnp.bfloat16),
            pltpu.VMEM(halves, jnp.bfloat16),
            pltpu.VMEM(boxes, jnp.bfloat16),
            pltpu.VMEM((2, BLOCKS, HEAD, BLOCK), jnp.bfloat16),
            pltpu.VMEM((2, BLOCKS, HEAD, BLOCK), jnp.bfloat16),
            pltpu.VMEM((2 * HALF, HEAD), jnp.float32),
            pltpu.VMEM((2, HEAD, 2 * HALF), jnp.float32),
            pltpu.VMEM((3,) + boxes, jnp.bfloat16),
            pltpu.VMEM((3,) + halves, jnp.bfloat16),
            pltpu.VMEM((2 * PEERS + groups // 2, HEADS, HEAD), jnp.float32),
            pltpu.VMEM((HEADS, HEAD), jnp.float32),
            pltpu.SemaphoreType.DMA((7,)),
            pltpu.SemaphoreType.DMA((8,)),
            pltpu.SemaphoreType.DMA((KINDS, 2)),
            pltpu.SemaphoreType.DMA((KINDS, 2)),
            pltpu.SemaphoreType.DMA((2, BLOCKS)),
            pltpu.SemaphoreType.REGULAR((8,)),
        ],
        compiler_params=pltpu.CompilerParams(
            collective_id=0, has_side_effects=True, vmem_limit_bytes=60 * 2**20
        ),
    )(
        lengths,
        *(
            array.reshape(halves)
            for array in (queries, key_vectors, value_vectors, gate_values, cotangent)
        ),
        norm_gain.reshape(1, width),
    )
    *grads, gain_total = pl.pallas_call(
        hand_over,
        out_shape=shapes,
        in_specs=[hbm] * 5,
        out_specs=(hbm,) * 5,
        scratch_shapes=[pltpu.VMEM(shape.shape, shape.dtype) for shape in shapes]
        + [pltpu.SemaphoreType.DMA((5,))] * 2,
        compiler_params=pltpu.CompilerParams(vmem_limit_bytes=60 * 2**20),
    )(*results)
    return *(array.reshape(row_count, width) for array in grads), gain_total.reshape(width)


def solution(mesh):
    rows = P(("dp", "ctx"), None)
    return jax.shard_map(
        body,
        mesh=mesh,
        in_specs=(rows,) * 5 + (P(), P("dp", None)),
        out_specs=(rows,) * 4 + (P(),),
        check_vma=False,
    )
```
